256 devices in a mesh: leaf: 32 (over x, z), heads: 2 (over core), dp: 4 (over y).
Axes of the slice: x: 4, y: 4, z: 8, core: 2. Of those that a mesh axis runs over, the one named last changes fastest.
Arguments:
- inputs: bfloat16 [128, 256, 8192], P(('dp', 'leaf'), None, 'heads'), parts along dimension 0, may hold values from -6 to 6
- dt_raw: float32 [128, 128, 256], P(('dp', 'leaf'), 'heads'), parts along dimension 0, may hold values from -3 to 7
- b_proj: bfloat16 [128, 256, 512], P(('dp', 'leaf'), None, 'heads'), parts along dimension 0, may hold values from -6 to 6
- c_proj: bfloat16 [128, 256, 512], P(('dp', 'leaf'), None, 'heads'), parts along dimension 0, may hold values from -6 to 6
- a_log: float32 [128], P('heads'), may hold values from -1.2 to 2.3
- dt_bias: float32 [128], P('heads'), may hold values from -6.5 to -5
- skip: float32 [128], P('heads'), may hold values from 0.5 to 1.5
- grad_out: bfloat16 [128, 256, 8192], P(('dp', 'leaf'), None, 'heads'), parts along dimension 0, may hold values from -6 to 6
- parent: int32 [128], P('dp'), parts along dimension 0, may hold values from -1 to 31, as said below
- children: int32 [128, 12], P('dp'), parts along dimension 0, may hold values from -1 to 31, as said below
Outputs:
- grad_inputs: bfloat16 [128, 256, 8192], P(('dp', 'leaf'), None, 'heads'), parts along dimension 0
- grad_dt: float32 [128, 128, 256], P(('dp', 'leaf'), 'heads'), parts along dimension 0
- grad_b: float32 [128, 256, 512], P(('dp', 'leaf'), None, 'heads'), parts along dimension 0
- grad_c: float32 [128, 256, 512], P(('dp', 'leaf'), None, 'heads'), parts along dimension 0
The draws below stay inside these ranges and needn't reach their ends.
There are 4 independent parts, one for each index of `dp`. The reference program is written for one: setup_inputs(seed, part) draws one part's arguments, and reference() takes and returns one part's arrays. A program takes and returns all parts, laid end to end along the dimension named above; an argument that names none is the same for every part. Nothing has to cross between parts.
Inputs may be any that keep to these rules, and one draw needn't show every extreme that they name: parent[n] is the segment whose end state starts segment n, -1 for the single root; every path from a segment up to the root holds at most 3 segments; some segment has exactly 12 children, and none has more. children[n] lists, in some order, every segment m with parent[m] = n, followed by -1 in the rest of its 12 entries.
All inputs are finite; a program needn't handle non-finite values.
Results may differ from the reference program's by a relative error of at most 0.012.
Values sent between devices are 32-bit elements; how exact they have to be, the bound alone decides.
A program may use at most 128 MiB of HBM per device.

```python
import jax
import jax.numpy as jnp
from jax import lax

RECURRENT_LANES = 128
GROUPS = 4
HEAD_DIM = 64
STATE = 128
H_BLOCK = 16
TREE_DEPTH = 3
SEG_LEN = 256
ROLLOUT_PIECES = 32
KIDS = 8
MAXCH = 12


def tree_tables(key):
    base = jax.random.fold_in(key, 29)
    key_perm, key_assign, key_coin, key_rank = jax.random.split(base, 4)
    node_ids = jnp.arange(ROLLOUT_PIECES, dtype=jnp.int32)
    if KIDS > 1:
        others = jax.random.randint(key_assign, (ROLLOUT_PIECES,), 2, KIDS + 1).astype(jnp.int32)
    else:
        others = jnp.ones((ROLLOUT_PIECES,), jnp.int32)
    grand = node_ids - (KIDS + 1)
    node_parent = jnp.where(node_ids == 0, -1, jnp.where(node_ids <= KIDS, 0, jnp.where(grand < MAXCH, 1, others))).astype(jnp.int32)
    if KIDS + 1 >= MAXCH:
        coin = jax.random.randint(key_coin, (), 0, 2).astype(jnp.int32)
        node_parent = jnp.where((grand == MAXCH - 1) & (coin == 1), 0, node_parent).astype(jnp.int32)
    slot = jax.random.permutation(key_perm, ROLLOUT_PIECES).astype(jnp.int32)
    parent_slot = jnp.where(node_parent < 0, -1, slot[jnp.maximum(node_parent, 0)]).astype(jnp.int32)
    parent_by_slot = jnp.zeros((ROLLOUT_PIECES,), jnp.int32).at[slot].set(parent_slot)
    score = jax.random.permutation(key_rank, ROLLOUT_PIECES).astype(jnp.int32)
    same = (node_parent[:, None] == node_parent[None, :]) & (score[None, :] < score[:, None])
    rank = jnp.sum(same.astype(jnp.int32), axis=1).astype(jnp.int32)
    row_of = jnp.where(node_parent < 0, ROLLOUT_PIECES, jnp.maximum(node_parent, 0)).astype(jnp.int32)
    lists = jnp.full((ROLLOUT_PIECES, MAXCH), -1, jnp.int32).at[row_of, rank].set(slot, mode='drop')
    children_by_slot = jnp.zeros((ROLLOUT_PIECES, MAXCH), jnp.int32).at[slot].set(lists)
    return (parent_by_slot, children_by_slot)


def draw_parent(key, part):
    return tree_tables(key)[0]


def draw_children(key, part):
    return tree_tables(key)[1]


def draw_dt_raw(key, part):
    jitter_seed, displacement_seed, place_seed, spike_seed = jax.random.split(jax.random.fold_in(key, 11), 4)
    shape = (ROLLOUT_PIECES, RECURRENT_LANES, SEG_LEN)
    gaussian_jitter = jnp.clip(0.5 * jax.random.normal(jitter_seed, shape, jnp.float32), -2.0, 2.0)
    displacement_value = jax.random.uniform(displacement_seed, (ROLLOUT_PIECES, 1, 1), jnp.float32, -0.7, 0.7)
    sequence_index = jax.random.randint(place_seed, (ROLLOUT_PIECES, 1, 1), 0, SEG_LEN)
    vocabulary_indices = jax.lax.broadcasted_iota(jnp.int32, shape, 2)
    spike_count = 5.5 + jax.random.uniform(spike_seed, (ROLLOUT_PIECES, RECURRENT_LANES, 1), jnp.float32, 0.0, 1.0)
    return jnp.where(vocabulary_indices == sequence_index, spike_count, gaussian_jitter + displacement_value)


def draw_a_log(key, part):
    pick = jax.random.fold_in(key, 13)
    return jax.random.uniform(pick, (RECURRENT_LANES,), jnp.float32, -1.2, 2.3)


def block_scale(stream_key, shape, shards, low, top_value):
    def one(axis_at, parts):
        draws = jax.random.uniform(jax.random.fold_in(jax.random.fold_in(stream_key, 6), axis_at), (parts,), jnp.float32, low / len(shards), top_value / len(shards))
        return jnp.repeat(jnp.exp(draws), shape[axis_at] // parts).reshape((-1,) + (1,) * (len(shape) - axis_at - 1))

    factor_of = one(*shards[0])
    for cut in shards[1:]:
        factor_of = factor_of * one(*cut)
    return factor_of


def scatter_about(rng, extent, width, limit, shards=(), kind=jnp.bfloat16):
    array = jax.random.normal(rng, extent, jnp.float32) * width
    if len(shards) > 0:
        array = block_scale(rng, extent, shards, -0.22, 0.18) * array
    return jnp.clip(array, min=-limit, max=limit).astype(kind)


def setup_inputs(seed: int = 0, part: int = 0) -> dict:
    key_list = jax.random.split(jax.random.key(seed), 11)
    own_keys = jax.random.split(jax.random.fold_in(key_list[10], part), 11)
    return {
        "inputs": scatter_about(own_keys[0], (ROLLOUT_PIECES, SEG_LEN, RECURRENT_LANES * HEAD_DIM), 1.0, 6.0, ((0, 32), (2, 2))),
        "dt_raw": draw_dt_raw(jax.random.fold_in(jax.random.fold_in(key_list[10], part), 71), part),
        "b_proj": scatter_about(own_keys[2], (ROLLOUT_PIECES, SEG_LEN, GROUPS * STATE), 1.0, 6.0, ((0, 32), (2, 2))),
        "c_proj": scatter_about(own_keys[3], (ROLLOUT_PIECES, SEG_LEN, GROUPS * STATE), 1.0, 6.0, ((0, 32), (2, 2))),
        "a_log": draw_a_log(jax.random.fold_in(key_list[10], 71), part),
        "dt_bias": jnp.clip(-6.5 + 1.5 * jax.random.uniform(key_list[5], (RECURRENT_LANES,), jnp.float32) ** block_scale(key_list[5], (RECURRENT_LANES,), ((0, 2),), -0.2, 0.2), -6.5, -5.0),
        "skip": jnp.clip(0.5 + 1.0 * jax.random.uniform(key_list[6], (RECURRENT_LANES,), jnp.float32) ** block_scale(key_list[6], (RECURRENT_LANES,), ((0, 2),), -0.2, 0.2), 0.5, 1.5),
        "grad_out": scatter_about(own_keys[7], (ROLLOUT_PIECES, SEG_LEN, RECURRENT_LANES * HEAD_DIM), 1.0, 6.0, ((0, 32), (2, 2))),
        "parent": draw_parent(jax.random.fold_in(jax.random.fold_in(key_list[10], part), 71), part),
        "children": draw_children(jax.random.fold_in(jax.random.fold_in(key_list[10], part), 71), part),
    }


highest = lax.Precision.HIGHEST

def lowered(values):
    return values.astype(jnp.bfloat16)

def prepare(raw_block, alog_block, bias_block):
    step_rate = jax.nn.softplus(raw_block + bias_block[:, None])
    total_log = jnp.cumsum(-jnp.exp(alog_block)[:, None] * step_rate, axis=1)
    return (step_rate, total_log)

def intra_terms(x_block, raw_block, b_block, c_block, alog_block, bias_block, skip_block):
    step_rate, total_log = prepare(raw_block, alog_block, bias_block)
    length = x_block.shape[0]
    row_index = lax.broadcasted_iota(jnp.int32, (length, length), 0)
    col_index = lax.broadcasted_iota(jnp.int32, (length, length), 1)
    causal = (row_index >= col_index)[None]
    log_gap = total_log[:, :, None] - total_log[:, None, :]
    decay_mat = jnp.where(causal, jnp.exp(jnp.where(causal, log_gap, 0.0)), 0.0)
    key_dot = jnp.dot(lowered(c_block), lowered(b_block).T, preferred_element_type=jnp.float32)
    mixing = lowered(decay_mat * key_dot[None] * step_rate[:, None, :])
    result = jnp.einsum('hts,shp->thp', mixing, lowered(x_block), preferred_element_type=jnp.float32)
    return result + skip_block[None, :, None] * x_block

def state_terms(x_block, raw_block, b_block, c_block, start_block, alog_block, bias_block):
    step_rate, total_log = prepare(raw_block, alog_block, bias_block)
    growth = jnp.exp(total_log)
    carried = growth.T[:, :, None] * jnp.einsum('tn,hpn->thp', c_block, start_block, precision=highest)
    tail_weight = jnp.exp(total_log[:, -1:] - total_log) * step_rate
    weighted = lowered(x_block * tail_weight.T[:, :, None])
    end_state = growth[:, -1][:, None, None] * start_block + jnp.einsum('shp,sn->hpn', weighted, lowered(b_block), preferred_element_type=jnp.float32)
    return (carried, end_state)

def summary(x_block, raw_block, b_block, c_block, dy_block, alog_block, bias_block):
    step_rate, total_log = prepare(raw_block, alog_block, bias_block)
    growth = jnp.exp(total_log)
    tail_weight = jnp.exp(total_log[:, -1:] - total_log) * step_rate
    weighted = lowered(x_block * tail_weight.T[:, :, None])
    local_end = jnp.einsum('shp,sn->hpn', weighted, lowered(b_block), preferred_element_type=jnp.float32)
    pulled_rows = lowered(dy_block * growth.T[:, :, None])
    pulled = jnp.einsum('thp,tn->hpn', pulled_rows, lowered(c_block), preferred_element_type=jnp.float32)
    return (local_end, growth[:, -1], pulled)

def whole_grads(x_block, raw_block, b_block, c_block, dy_block, start_block, grad_block, alog_block, bias_block, skip_block):

    def combined(x_in, raw_in, b_in, c_in):
        carried, end_state = state_terms(x_in, raw_in, b_in, c_in, start_block, alog_block, bias_block)
        return (intra_terms(x_in, raw_in, b_in, c_in, alog_block, bias_block, skip_block) + carried, end_state)
    unused, pullback = jax.vjp(combined, x_block, raw_block, b_block, c_block)
    return pullback((dy_block, grad_block))

def forward_tree(own_end, carries, link_up):
    node_count = own_end.shape[0]
    start_state = jnp.zeros_like(own_end)
    for depth_step in range(TREE_DEPTH - 1):
        finish = carries * start_state + own_end
        start_state = jnp.dot(link_up, finish.reshape(node_count, -1), precision=highest).reshape(own_end.shape)
    return start_state

def backward_tree(own_pull, carries, link_down):
    node_count = own_pull.shape[0]
    end_grad = jnp.zeros_like(own_pull)
    for depth_step in range(TREE_DEPTH - 1):
        start_grad = own_pull + carries * end_grad
        end_grad = jnp.dot(link_down, start_grad.reshape(node_count, -1), precision=highest).reshape(own_pull.shape)
    return end_grad

def reference(inputs, dt_raw, b_proj, c_proj, a_log, dt_bias, skip, grad_out, parent, children):
    blocks = RECURRENT_LANES // H_BLOCK
    per_group = blocks // GROUPS
    state_size = HEAD_DIM * STATE
    alog_blocks = a_log.reshape(blocks, H_BLOCK)
    bias_blocks = dt_bias.reshape(blocks, H_BLOCK)
    skip_blocks = skip.reshape(blocks, H_BLOCK)

    def split_node(x_node, raw_node, b_node, c_node, dy_node):
        x_blocks = x_node.reshape(SEG_LEN, blocks, H_BLOCK, HEAD_DIM).transpose(1, 0, 2, 3).astype(jnp.float32)
        dy_blocks = dy_node.reshape(SEG_LEN, blocks, H_BLOCK, HEAD_DIM).transpose(1, 0, 2, 3).astype(jnp.float32)
        raw_blocks = raw_node.reshape(blocks, H_BLOCK, SEG_LEN)
        b_blocks = jnp.repeat(b_node.reshape(SEG_LEN, GROUPS, STATE).transpose(1, 0, 2), per_group, axis=0).astype(jnp.float32)
        c_blocks = jnp.repeat(c_node.reshape(SEG_LEN, GROUPS, STATE).transpose(1, 0, 2), per_group, axis=0).astype(jnp.float32)
        return (x_blocks, raw_blocks, b_blocks, c_blocks, dy_blocks)

    def first_node(members):
        x_blocks, raw_blocks, b_blocks, c_blocks, dy_blocks = split_node(members[0], members[1], members[2], members[3], members[4])

        def first_block(block_in):
            return summary(block_in[0], block_in[1], block_in[2], block_in[3], block_in[4], block_in[5], block_in[6])
        return lax.map(first_block, (x_blocks, raw_blocks, b_blocks, c_blocks, dy_blocks, alog_blocks, bias_blocks))
    own_end, carries, own_pull = lax.map(first_node, (inputs, dt_raw, b_proj, c_proj, grad_out))
    own_end = own_end.reshape(ROLLOUT_PIECES, RECURRENT_LANES, state_size)
    own_pull = own_pull.reshape(ROLLOUT_PIECES, RECURRENT_LANES, state_size)
    carries = carries.reshape(ROLLOUT_PIECES, RECURRENT_LANES, 1)
    node_ids = jnp.arange(ROLLOUT_PIECES, dtype=jnp.int32)
    link_up = (parent[:, None] == node_ids[None, :]).astype(jnp.float32)
    link_down = jnp.any(children[:, :, None] == node_ids[None, None, :], axis=1).astype(jnp.float32)
    start_state = forward_tree(own_end, carries, link_up).reshape(ROLLOUT_PIECES, blocks, H_BLOCK, HEAD_DIM, STATE)
    end_grad = backward_tree(own_pull, carries, link_down).reshape(ROLLOUT_PIECES, blocks, H_BLOCK, HEAD_DIM, STATE)

    def second_node(members):
        x_blocks, raw_blocks, b_blocks, c_blocks, dy_blocks = split_node(members[0], members[1], members[2], members[3], members[4])

        def second_block(block_in):
            return whole_grads(block_in[0], block_in[1], block_in[2], block_in[3], block_in[4], block_in[5], block_in[6], block_in[7], block_in[8], block_in[9])
        return lax.map(second_block, (x_blocks, raw_blocks, b_blocks, c_blocks, dy_blocks, members[5], members[6], alog_blocks, bias_blocks, skip_blocks))
    grad_x, grad_raw, grad_bb, grad_cb = lax.map(second_node, (inputs, dt_raw, b_proj, c_proj, grad_out, start_state, end_grad))
    grad_inputs = grad_x.transpose(0, 2, 1, 3, 4).reshape(ROLLOUT_PIECES, SEG_LEN, RECURRENT_LANES * HEAD_DIM).astype(jnp.bfloat16)
    grad_dt = grad_raw.reshape(ROLLOUT_PIECES, RECURRENT_LANES, SEG_LEN)
    grad_b = grad_bb.reshape(ROLLOUT_PIECES, GROUPS, per_group, SEG_LEN, STATE).sum(axis=2).transpose(0, 2, 1, 3).reshape(ROLLOUT_PIECES, SEG_LEN, GROUPS * STATE)
    grad_c = grad_cb.reshape(ROLLOUT_PIECES, GROUPS, per_group, SEG_LEN, STATE).sum(axis=2).transpose(0, 2, 1, 3).reshape(ROLLOUT_PIECES, SEG_LEN, GROUPS * STATE)
    return (grad_inputs, grad_dt, grad_b, grad_c)
```

```python
import functools

import jax
import jax.numpy as jnp
from jax import lax
from jax.experimental import pallas as pl
from jax.experimental.pallas import tpu as pltpu
from jax.sharding import PartitionSpec as P

HEAD_DIM = 64
STATE = 128
BLOCK = 8
TREE_DEPTH = 3
F32 = jnp.float32
BF16 = jnp.bfloat16

highest = lax.Precision.HIGHEST


def dot(a, b, da=1, db=0):
    return lax.dot_general(a, b, (((da,), (db,)), ((), ())), preferred_element_type=F32)


def prefix(rows, ones):
    top = rows.astype(BF16)
    rest = rows - top.astype(F32)
    mid = rest.astype(BF16)
    low = (rest - mid.astype(F32)).astype(BF16)
    return dot(top, ones) + (dot(mid, ones) + dot(low, ones))


def triangle(n, lower):
    r = lax.broadcasted_iota(jnp.int32, (n, n), 0)
    c = lax.broadcasted_iota(jnp.int32, (n, n), 1)
    return jnp.where(r >= c if lower else r <= c, 1.0, 0.0).astype(BF16)


def rates(raw, alog, bias):
    v = raw + bias
    rate = jnp.maximum(v, 0.0) + jnp.log1p(jnp.exp(-jnp.abs(v)))
    cum = prefix(-jnp.exp(alog) * rate, triangle(raw.shape[1], False))
    return rate, cum


def spread(rows, flat):
    h, t = rows.shape
    return (flat.astype(F32).reshape(h, -1, t) * rows[:, None, :]).reshape(flat.shape)


def fold(flat, heads):
    return flat.reshape(heads, -1, flat.shape[1]).sum(axis=1)


def first_kernel(x_ref, dy_ref, raw_ref, b_ref, c_ref, alog_ref, bias_ref, end_ref, pull_ref, carry_ref, xt_ref, dyt_ref):
    rate, cum = rates(raw_ref[...], alog_ref[...], bias_ref[...])
    last = cum[:, -1:]
    tail = jnp.exp(last - cum) * rate
    growth = jnp.exp(cum)
    xt = x_ref[...].T
    dyt = dy_ref[...].T
    xt_ref[...] = xt
    dyt_ref[...] = dyt
    end_ref[...] = dot(spread(tail, xt).astype(BF16), b_ref[...])
    pull_ref[...] = dot(spread(growth, dyt).astype(BF16), c_ref[...])
    carry_ref[...] = jnp.broadcast_to(jnp.exp(last), carry_ref.shape)


def inner_kernel(per, dy_ref, raw_ref, b_ref, c_ref, alog_ref, bias_ref, skip_ref, xt_ref, dyt_ref, dx_ref, row_ref, col_ref, dbt_ref, dct_ref, score, total):
    t = raw_ref.shape[1]
    half = t // 2
    step = pl.program_id(0)

    @pl.when(step % per == 0)
    def _():
        score[...] = dot(c_ref[...], b_ref[...], 1, 1)
        total[...] = jnp.zeros_like(total)

    rate, cum = rates(raw_ref[...], alog_ref[...], bias_ref[...])
    rowterm = jnp.log(rate) - cum
    cumt = cum.T
    r = lax.broadcasted_iota(jnp.int32, (half, half), 0)
    c = lax.broadcasted_iota(jnp.int32, (half, half), 1)
    causal = r >= c
    lane = lax.broadcasted_iota(jnp.int32, (2 * HEAD_DIM, t), 0)
    lefts = []
    for i in range(BLOCK):
        pair = slice(i // 2 * 2 * HEAD_DIM, (i // 2 + 1) * 2 * HEAD_DIM)
        mine = slice(i * HEAD_DIM, (i + 1) * HEAD_DIM)
        xpair = xt_ref[pair, :]
        xhead = jnp.where((lane // HEAD_DIM) == i % 2, xpair, jnp.zeros_like(xpair))
        dyh = dyt_ref[mine, :]
        skip = skip_ref[i:i + 1, :]
        parts = {}
        for a, b in ((0, 0), (1, 0), (1, 1)):
            rows = slice(a * half, (a + 1) * half)
            cols = slice(b * half, (b + 1) * half)
            gap = cumt[rows, i:i + 1] + rowterm[i:i + 1, cols]
            if a == b:
                gap = jnp.where(causal, gap, -1e30)
            decay = jnp.exp(gap)
            mix = decay * score[rows, cols]
            dmix = dot(dy_ref[rows, pair], xhead[:, cols])
            total[rows, cols] += dmix * decay
            parts[a, b] = (mix.astype(BF16), dmix * mix)
        q0, q1, q2 = parts[0, 0][1], parts[1, 0][1], parts[1, 1][1]
        col_ref[i:i + 1, :half] = jnp.sum(q0 + q1, axis=0, keepdims=True)
        col_ref[i:i + 1, half:] = jnp.sum(q2, axis=0, keepdims=True)
        lefts.append(jnp.concatenate([jnp.sum(q0, axis=1, keepdims=True), jnp.sum(q1 + q2, axis=1, keepdims=True)], axis=0))
        left = jnp.concatenate([parts[0, 0][0], parts[1, 0][0]], axis=0)
        dx_ref[mine, :half] = dot(dyh, left) + skip * dyh[:, :half].astype(F32)
        dx_ref[mine, half:] = dot(dyh[:, half:], parts[1, 1][0]) + skip * dyh[:, half:].astype(F32)
    row_ref[...] = jnp.concatenate(lefts, axis=1).T

    @pl.when(step % per == per - 1)
    def _():
        summed = jnp.where(
            lax.broadcasted_iota(jnp.int32, (t, t), 0) >= lax.broadcasted_iota(jnp.int32, (t, t), 1), total[...], 0.0
        ).astype(BF16)
        dbt_ref[...] = dot(c_ref[...], summed, 0, 0)
        dct_ref[...] = dot(b_ref[...], summed, 0, 1)


def last_kernel(per, raw_ref, b_ref, c_ref, alog_ref, bias_ref, xt_ref, dyt_ref, start_ref, grad_ref, dx_ref, row_ref, col_ref, dbt_ref, dct_ref, gx_ref, gdt_ref, gb_ref, gc_ref, sumb, sumc):
    step = pl.program_id(0)
    t = raw_ref.shape[1]

    @pl.when(step % per == 0)
    def _():
        sumb[...] = dbt_ref[...]
        sumc[...] = dct_ref[...]

    v = raw_ref[...] + bias_ref[...]
    rate, cum = rates(raw_ref[...], alog_ref[...], bias_ref[...])
    last = cum[:, -1:]
    growth = jnp.exp(cum)
    tail = jnp.exp(last - cum) * rate
    start = start_ref[...]
    grad = grad_ref[...]
    inner = jnp.sum(fold(start * grad, BLOCK), axis=1, keepdims=True)
    start_low = start.astype(BF16)
    grad_low = grad.astype(BF16)
    xt = xt_ref[...]
    dyt = dyt_ref[...]
    pulled = dot(grad_low, b_ref[...], 1, 1)
    z = fold(xt.astype(F32) * pulled, BLOCK) * tail
    gx_ref[...] = (dx_ref[...] + spread(tail, pulled)).astype(BF16).T
    sumb[...] += dot(grad_low, spread(tail, xt).astype(BF16), 0, 0)
    carried = dot(start_low, c_ref[...], 1, 1)
    g = fold(dyt.astype(F32) * carried, BLOCK) * growth
    sumc[...] += dot(start_low, spread(growth, dyt).astype(BF16), 0, 0)
    col = col_ref[...]
    dcum = row_ref[...] - col + g - z
    at_end = jnp.sum(z, axis=1, keepdims=True) + growth[:, -1:] * inner
    dlog = prefix(dcum, triangle(t, True)) + at_end
    slope = 1.0 / (1.0 + jnp.exp(-v))
    gdt_ref[...] = ((col + z) / rate - jnp.exp(alog_ref[...]) * dlog) * slope

    @pl.when(step % per == per - 1)
    def _():
        gb_ref[...] = sumb[...].T
        gc_ref[...] = sumc[...].T


def specs(per, t):
    flat = pl.BlockSpec((BLOCK * HEAD_DIM, t), lambda i: (i, 0))
    return {
        "nat": pl.BlockSpec((t, BLOCK * HEAD_DIM), lambda i: (0, i)),
        "rows": pl.BlockSpec((BLOCK, t), lambda i: (i, 0)),
        "group": pl.BlockSpec((t, STATE), lambda i: (0, i // per)),
        "one": pl.BlockSpec((BLOCK, 1), lambda i: (i, 0)),
        "flat": flat,
        "state": pl.BlockSpec((BLOCK * HEAD_DIM, STATE), lambda i: (i, 0)),
        "lane": pl.BlockSpec((BLOCK, STATE), lambda i: (i, 0)),
        "groupt": pl.BlockSpec((STATE, t), lambda i: (i // per, 0)),
    }


def params(mib):
    return pltpu.CompilerParams(vmem_limit_bytes=mib << 20)


def sds(shape, kind=F32):
    return jax.ShapeDtypeStruct(shape, kind)


def summaries(x, dy, raw, b, c, alog, bias, per):
    heads, t = raw.shape
    s = specs(per, t)
    return pl.pallas_call(
        first_kernel,
        grid=(heads // BLOCK,),
        in_specs=[s["nat"], s["nat"], s["rows"], s["group"], s["group"], s["one"], s["one"]],
        out_specs=[s["state"], s["state"], s["lane"], s["flat"], s["flat"]],
        out_shape=[
            sds((heads * HEAD_DIM, STATE)),
            sds((heads * HEAD_DIM, STATE)),
            sds((heads, STATE)),
            sds((heads * HEAD_DIM, t), BF16),
            sds((heads * HEAD_DIM, t), BF16),
        ],
        compiler_params=params(32),
        name="summaries",
    )(x, dy, raw, b, c, alog, bias)


def inner_grads(dy, raw, b, c, alog, bias, skip, xt, dyt, per):
    heads, t = raw.shape
    s = specs(per, t)
    groups = heads // BLOCK // per
    return pl.pallas_call(
        functools.partial(inner_kernel, per),
        grid=(heads // BLOCK,),
        in_specs=[s["nat"], s["rows"], s["group"], s["group"], s["one"], s["one"], s["one"], s["flat"], s["flat"]],
        out_specs=[s["flat"], s["rows"], s["rows"], s["groupt"], s["groupt"]],
        out_shape=[
            sds((heads * HEAD_DIM, t)),
            sds((heads, t)),
            sds((heads, t)),
            sds((groups * STATE, t)),
            sds((groups * STATE, t)),
        ],
        scratch_shapes=[pltpu.VMEM((t, t), F32), pltpu.VMEM((t, t), F32)],
        compiler_params=params(32),
        cost_estimate=pl.CostEstimate(flops=heads * t * t * 256, bytes_accessed=heads * t * 512, transcendentals=heads * t * t),
        name="inner_grads",
    )(dy, raw, b, c, alog, bias, skip, xt, dyt)


def final_grads(raw, b, c, alog, bias, xt, dyt, start, grad, inner, per):
    heads, t = raw.shape
    s = specs(per, t)
    groups = heads // BLOCK // per
    return pl.pallas_call(
        functools.partial(last_kernel, per),
        grid=(heads // BLOCK,),
        in_specs=[s["rows"], s["group"], s["group"], s["one"], s["one"], s["flat"], s["flat"], s["state"], s["state"], s["flat"], s["rows"], s["rows"], s["groupt"], s["groupt"]],
        out_specs=[s["nat"], s["rows"], s["group"], s["group"]],
        out_shape=[
            sds((t, heads * HEAD_DIM), BF16),
            sds((heads, t)),
            sds((t, groups * STATE)),
            sds((t, groups * STATE)),
        ],
        scratch_shapes=[pltpu.VMEM((STATE, t), F32), pltpu.VMEM((STATE, t), F32)],
        compiler_params=params(32),
        name="final_grads",
    )(raw, b, c, alog, bias, xt, dyt, start, grad, *inner)


def forward_tree(own_end, carries, link_up):
    node_count = own_end.shape[0]
    start_state = jnp.zeros_like(own_end)
    for depth_step in range(TREE_DEPTH - 1):
        finish = carries * start_state + own_end
        start_state = jnp.dot(link_up, finish.reshape(node_count, -1), precision=highest).reshape(own_end.shape)
    return start_state


def backward_tree(own_pull, carries, link_down):
    node_count = own_pull.shape[0]
    end_grad = jnp.zeros_like(own_pull)
    for depth_step in range(TREE_DEPTH - 1):
        start_grad = own_pull + carries * end_grad
        end_grad = jnp.dot(link_down, start_grad.reshape(node_count, -1), precision=highest).reshape(own_pull.shape)
    return end_grad


def exchange(payload):
    return lax.all_to_all(payload, "leaf", split_axis=0, concat_axis=0, tiled=True)


def body(inputs, dt_raw, b_proj, c_proj, a_log, dt_bias, skip, grad_out, parent, children):
    heads = a_log.shape[0]
    groups = b_proj.shape[2] // STATE
    per = heads // BLOCK // groups
    nodes = parent.shape[0]
    x, dy, raw, b, c = inputs[0], grad_out[0], dt_raw[0], b_proj[0], c_proj[0]
    alog, bias, skips = a_log[:, None], dt_bias[:, None], skip[:, None]
    own_end, own_pull, carry, xt, dyt = summaries(x, dy, raw, b, c, alog, bias, per)
    node_ids = jnp.arange(nodes, dtype=jnp.int32)
    link_up = (parent[:, None] == node_ids[None, :]).astype(F32)
    link_down = jnp.any(children[:, :, None] == node_ids[None, None, :], axis=1).astype(F32)

    share = heads // nodes

    def as_slices(flat):
        return flat.reshape(nodes, share * HEAD_DIM, STATE)

    carry_slices = jnp.repeat(exchange(carry).reshape(nodes, share, STATE), HEAD_DIM, axis=1)
    start_slices = forward_tree(as_slices(exchange(own_end)), carry_slices, link_up)
    start = exchange(start_slices.reshape(heads * HEAD_DIM, STATE))
    inner = inner_grads(dy, raw, b, c, alog, bias, skips, xt, dyt, per)
    grad_slices = backward_tree(as_slices(exchange(own_pull)), carry_slices, link_down)
    grad = exchange(grad_slices.reshape(heads * HEAD_DIM, STATE))
    gx, gdt, gb, gc = final_grads(raw, b, c, alog, bias, xt, dyt, start, grad, inner, per)
    return gx[None], gdt[None], gb[None], gc[None]


def solution(mesh):
    placed = (
        P(("dp", "leaf"), None, "heads"),
        P(("dp", "leaf"), "heads", None),
        P(("dp", "leaf"), None, "heads"),
        P(("dp", "leaf"), None, "heads"),
        P("heads"),
        P("heads"),
        P("heads"),
        P(("dp", "leaf"), None, "heads"),
        P("dp"),
        P("dp", None),
    )
    return jax.shard_map(
        body,
        mesh=mesh,
        in_specs=placed,
        out_specs=(
            P(("dp", "leaf"), None, "heads"),
            P(("dp", "leaf"), "heads", None),
            P(("dp", "leaf"), None, "heads"),
            P(("dp", "leaf"), None, "heads"),
        ),
        check_vma=False,
    )
```

```python
import functools

import jax
import jax.numpy as jnp
from jax import lax
from jax.experimental import pallas as pl
from jax.experimental.pallas import tpu as pltpu
from jax.sharding import PartitionSpec as P

HEAD_DIM = 64
STATE = 128
BLOCK = 8
NX = 4
NZ = 8
ARM = 4
LAG = 2
F32 = jnp.float32
BF16 = jnp.bfloat16

MESH = pl.DeviceIdType.MESH


def dot(a, b, da=1, db=0):
    return lax.dot_general(a, b, (((da,), (db,)), ((), ())), preferred_element_type=F32)


def prefix(rows, ones):
    top = rows.astype(BF16)
    rest = rows - top.astype(F32)
    mid = rest.astype(BF16)
    low = (rest - mid.astype(F32)).astype(BF16)
    return dot(top, ones) + (dot(mid, ones) + dot(low, ones))


def triangle(n, lower):
    r = lax.broadcasted_iota(jnp.int32, (n, n), 0)
    c = lax.broadcasted_iota(jnp.int32, (n, n), 1)
    return jnp.where(r >= c if lower else r <= c, 1.0, 0.0).astype(BF16)


def rates(raw, alog, bias):
    v = raw + bias
    rate = jnp.maximum(v, 0.0) + jnp.log1p(jnp.exp(-jnp.abs(v)))
    cum = prefix(-jnp.exp(alog) * rate, triangle(raw.shape[1], False))
    return rate, cum


def spread(rows, flat):
    h, t = rows.shape
    return (flat.astype(F32).reshape(h, -1, t) * rows[:, None, :]).reshape(flat.shape)


def fold(flat, heads):
    return flat.reshape(heads, -1, flat.shape[1]).sum(axis=1)


def first_kernel(x_ref, dy_ref, raw_ref, b_ref, c_ref, alog_ref, bias_ref, own_ref, carry_ref, xt_ref, dyt_ref):
    rate, cum = rates(raw_ref[...], alog_ref[...], bias_ref[...])
    last = cum[:, -1:]
    tail = jnp.exp(last - cum) * rate
    growth = jnp.exp(cum)
    xt = x_ref[...].T
    dyt = dy_ref[...].T
    xt_ref[...] = xt
    dyt_ref[...] = dyt
    end = dot(spread(tail, xt).astype(BF16), b_ref[...])
    pull = dot(spread(growth, dyt).astype(BF16), c_ref[...])
    own_ref[:, 0] = end.reshape(BLOCK, HEAD_DIM, STATE)
    own_ref[:, 1] = pull.reshape(BLOCK, HEAD_DIM, STATE)
    carry_ref[...] = jnp.broadcast_to(jnp.exp(last), carry_ref.shape)


def inner_kernel(per, dy_ref, raw_ref, b_ref, c_ref, alog_ref, bias_ref, skip_ref, xt_ref, dyt_ref, dx_ref, row_ref, col_ref, dbt_ref, dct_ref, score, total):
    t = raw_ref.shape[1]
    half = t // 2
    step = pl.program_id(0)

    @pl.when(step % per == 0)
    def _():
        score[...] = dot(c_ref[...], b_ref[...], 1, 1)
        total[...] = jnp.zeros_like(total)

    rate, cum = rates(raw_ref[...], alog_ref[...], bias_ref[...])
    rowterm = jnp.log(rate) - cum
    cumt = cum.T
    r = lax.broadcasted_iota(jnp.int32, (half, half), 0)
    c = lax.broadcasted_iota(jnp.int32, (half, half), 1)
    causal = r >= c
    lane = lax.broadcasted_iota(jnp.int32, (2 * HEAD_DIM, t), 0)
    lefts = []
    for i in range(BLOCK):
        pair = slice(i // 2 * 2 * HEAD_DIM, (i // 2 + 1) * 2 * HEAD_DIM)
        mine = slice(i * HEAD_DIM, (i + 1) * HEAD_DIM)
        xpair = xt_ref[pair, :]
        xhead = jnp.where((lane // HEAD_DIM) == i % 2, xpair, jnp.zeros_like(xpair))
        dyh = dyt_ref[mine, :]
        skip = skip_ref[i:i + 1, :]
        parts = {}
        for a, b in ((0, 0), (1, 0), (1, 1)):
            rows = slice(a * half, (a + 1) * half)
            cols = slice(b * half, (b + 1) * half)
            gap = cumt[rows, i:i + 1] + rowterm[i:i + 1, cols]
            if a == b:
                gap = jnp.where(causal, gap, -1e30)
            decay = jnp.exp(gap)
            mix = decay * score[rows, cols]
            dmix = dot(dy_ref[rows, pair], xhead[:, cols])
            total[rows, cols] += dmix * decay
            parts[a, b] = (mix.astype(BF16), dmix * mix)
        q0, q1, q2 = parts[0, 0][1], parts[1, 0][1], parts[1, 1][1]
        col_ref[i:i + 1, :half] = jnp.sum(q0 + q1, axis=0, keepdims=True)
        col_ref[i:i + 1, half:] = jnp.sum(q2, axis=0, keepdims=True)
        lefts.append(jnp.concatenate([jnp.sum(q0, axis=1, keepdims=True), jnp.sum(q1 + q2, axis=1, keepdims=True)], axis=0))
        left = jnp.concatenate([parts[0, 0][0], parts[1, 0][0]], axis=0)
        dx_ref[mine, :half] = dot(dyh, left) + skip * dyh[:, :half].astype(F32)
        dx_ref[mine, half:] = dot(dyh[:, half:], parts[1, 1][0]) + skip * dyh[:, half:].astype(F32)
    row_ref[...] = jnp.concatenate(lefts, axis=1).T

    @pl.when(step % per == per - 1)
    def _():
        summed = jnp.where(
            lax.broadcasted_iota(jnp.int32, (t, t), 0) >= lax.broadcasted_iota(jnp.int32, (t, t), 1), total[...], 0.0
        ).astype(BF16)
        dbt_ref[...] = dot(c_ref[...], summed, 0, 0)
        dct_ref[...] = dot(b_ref[...], summed, 0, 1)


def last_kernel(per, raw_ref, b_ref, c_ref, alog_ref, bias_ref, xt_ref, dyt_ref, both_ref, dx_ref, row_ref, col_ref, dbt_ref, dct_ref, gx_ref, gdt_ref, gb_ref, gc_ref, sumb, sumc):
    step = pl.program_id(0)
    t = raw_ref.shape[1]

    @pl.when(step % per == 0)
    def _():
        sumb[...] = dbt_ref[...]
        sumc[...] = dct_ref[...]

    v = raw_ref[...] + bias_ref[...]
    rate, cum = rates(raw_ref[...], alog_ref[...], bias_ref[...])
    last = cum[:, -1:]
    growth = jnp.exp(cum)
    tail = jnp.exp(last - cum) * rate
    start = both_ref[:, 0].reshape(BLOCK * HEAD_DIM, STATE)
    grad = both_ref[:, 1].reshape(BLOCK * HEAD_DIM, STATE)
    inner = jnp.sum(fold(start * grad, BLOCK), axis=1, keepdims=True)
    start_low = start.astype(BF16)
    grad_low = grad.astype(BF16)
    xt = xt_ref[...]
    dyt = dyt_ref[...]
    pulled = dot(grad_low, b_ref[...], 1, 1)
    z = fold(xt.astype(F32) * pulled, BLOCK) * tail
    gx_ref[...] = (dx_ref[...] + spread(tail, pulled)).astype(BF16).T
    sumb[...] += dot(grad_low, spread(tail, xt).astype(BF16), 0, 0)
    carried = dot(start_low, c_ref[...], 1, 1)
    g = fold(dyt.astype(F32) * carried, BLOCK) * growth
    sumc[...] += dot(start_low, spread(growth, dyt).astype(BF16), 0, 0)
    col = col_ref[...]
    dcum = row_ref[...] - col + g - z
    at_end = jnp.sum(z, axis=1, keepdims=True) + growth[:, -1:] * inner
    dlog = prefix(dcum, triangle(t, True)) + at_end
    slope = 1.0 / (1.0 + jnp.exp(-v))
    gdt_ref[...] = ((col + z) / rate - jnp.exp(alog_ref[...]) * dlog) * slope

    @pl.when(step % per == per - 1)
    def _():
        gb_ref[...] = sumb[...].T
        gc_ref[...] = sumc[...].T


def specs(per, t):
    flat = pl.BlockSpec((BLOCK * HEAD_DIM, t), lambda i: (i, 0))
    return {
        "nat": pl.BlockSpec((t, BLOCK * HEAD_DIM), lambda i: (0, i)),
        "rows": pl.BlockSpec((BLOCK, t), lambda i: (i, 0)),
        "group": pl.BlockSpec((t, STATE), lambda i: (0, i // per)),
        "one": pl.BlockSpec((BLOCK, 1), lambda i: (i, 0)),
        "flat": flat,
        "state": pl.BlockSpec((BLOCK, 2, HEAD_DIM, STATE), lambda i: (i, 0, 0, 0)),
        "lane": pl.BlockSpec((BLOCK, STATE), lambda i: (i, 0)),
        "groupt": pl.BlockSpec((STATE, t), lambda i: (i // per, 0)),
    }


def params(mib):
    return pltpu.CompilerParams(vmem_limit_bytes=mib << 20)


def sds(shape, kind=F32):
    return jax.ShapeDtypeStruct(shape, kind)


def summaries(x, dy, raw, b, c, alog, bias, per):
    heads, t = raw.shape
    s = specs(per, t)
    return pl.pallas_call(
        first_kernel,
        grid=(heads // BLOCK,),
        in_specs=[s["nat"], s["nat"], s["rows"], s["group"], s["group"], s["one"], s["one"]],
        out_specs=[s["state"], s["lane"], s["flat"], s["flat"]],
        out_shape=[
            sds((heads, 2, HEAD_DIM, STATE)),
            sds((heads, STATE)),
            sds((heads * HEAD_DIM, t), BF16),
            sds((heads * HEAD_DIM, t), BF16),
        ],
        compiler_params=params(32),
        name="summaries",
    )(x, dy, raw, b, c, alog, bias)


def inner_grads(dy, raw, b, c, alog, bias, skip, xt, dyt, per):
    heads, t = raw.shape
    s = specs(per, t)
    groups = heads // BLOCK // per
    return pl.pallas_call(
        functools.partial(inner_kernel, per),
        grid=(heads // BLOCK,),
        in_specs=[s["nat"], s["rows"], s["group"], s["group"], s["one"], s["one"], s["one"], s["flat"], s["flat"]],
        out_specs=[s["flat"], s["rows"], s["rows"], s["groupt"], s["groupt"]],
        out_shape=[
            sds((heads * HEAD_DIM, t)),
            sds((heads, t)),
            sds((heads, t)),
            sds((groups * STATE, t)),
            sds((groups * STATE, t)),
        ],
        scratch_shapes=[pltpu.VMEM((t, t), F32), pltpu.VMEM((t, t), F32)],
        compiler_params=params(32),
        cost_estimate=pl.CostEstimate(flops=heads * t * t * 256, bytes_accessed=heads * t * 512, transcendentals=heads * t * t),
        name="inner_grads",
    )(dy, raw, b, c, alog, bias, skip, xt, dyt)


def final_grads(raw, b, c, alog, bias, xt, dyt, both, inner, per):
    heads, t = raw.shape
    s = specs(per, t)
    groups = heads // BLOCK // per
    return pl.pallas_call(
        functools.partial(last_kernel, per),
        grid=(heads // BLOCK,),
        in_specs=[s["rows"], s["group"], s["group"], s["one"], s["one"], s["flat"], s["flat"], s["state"], s["flat"], s["rows"], s["rows"], s["groupt"], s["groupt"]],
        out_specs=[s["nat"], s["rows"], s["group"], s["group"]],
        out_shape=[
            sds((t, heads * HEAD_DIM), BF16),
            sds((heads, t)),
            sds((t, groups * STATE)),
            sds((t, groups * STATE)),
        ],
        scratch_shapes=[pltpu.VMEM((STATE, t), F32), pltpu.VMEM((STATE, t), F32)],
        compiler_params=params(32),
        name="final_grads",
    )(raw, b, c, alog, bias, xt, dyt, both, *inner)


def arms(near, pick):
    def furthest(v):
        return jnp.max(jnp.where(near, v, 0), axis=1, keepdims=True)

    up = furthest(jnp.where(pick < ARM, pick, 0))
    down = furthest(jnp.where(pick > ARM, NZ - pick, 0))
    both = furthest(jnp.where(pick == ARM, 1, 0)) > 0
    return jnp.where(both & (up >= down), ARM, up), jnp.where(both & (up < down), ARM, down)


def tree_kernel(slots, parent_ref, carry_ref, own_ref, both_ref, xin, extra, got, put, res, crow, carried, scale, relay, local, remote, here,
                own_sem, in_send, in_recv, z_send, z_recv, out_send, out_recv, out_own, carry_send, carry_recv):
    nodes = NX * NZ
    part = own_ref.shape[0] // NX
    half = HEAD_DIM // 2
    chunks = part * 2
    rounds = chunks + LAG * (ARM - 1)
    ahead = 3
    me = lax.axis_index("leaf")
    x, z = me // NZ, lax.rem(me, NZ)

    def peer(k):
        return lax.rem(x + k, NX)

    def at(px, pz):
        return {"leaf": px * NZ + pz}

    barrier = pltpu.get_barrier_semaphore()

    @pl.loop(1, nodes)
    def _(k):
        pl.semaphore_signal(barrier, inc=1, device_id={"leaf": lax.rem(me + k, nodes)}, device_id_type=MESH)

    crow[...] = jnp.zeros_like(crow)
    crow[0, :, : carry_ref.shape[0]] = carry_ref[...].T[0:1, :]
    got[:, 0:LAG] = jnp.zeros((2, LAG) + got.shape[2:], F32)
    pl.semaphore_wait(barrier, nodes - 1)

    def in_copy(hd, k):
        return pltpu.make_async_remote_copy(
            src_ref=own_ref.at[peer(k) * part + hd],
            dst_ref=xin.at[x, hd],
            send_sem=in_send.at[hd, k - 1],
            recv_sem=in_recv.at[hd, k - 1],
            device_id=at(peer(k), z),
            device_id_type=MESH,
        )

    def start_in(hd):
        for k in range(1, NX):
            in_copy(hd, k).start()

    own_copy = pltpu.make_async_copy(own_ref.at[pl.ds(x * part, part)], xin.at[x], own_sem)
    own_copy.start()
    start_in(0)

    def carry_copy(k):
        return pltpu.make_async_remote_copy(
            src_ref=crow.at[0],
            dst_ref=carried.at[me],
            send_sem=carry_send,
            recv_sem=carry_recv,
            device_id={"leaf": lax.rem(me + k, nodes)},
            device_id_type=MESH,
        )

    @pl.loop(1, nodes)
    def _(k):
        carry_copy(k).start()

    for hd in range(1, ahead):
        start_in(hd)

    lanes = 128
    sub = lax.broadcasted_iota(jnp.int32, (nodes, lanes), 0)
    lane = lax.broadcasted_iota(jnp.int32, (nodes, lanes), 1)
    par_col = jnp.full((nodes, lanes), -1, jnp.int32)
    par_row = jnp.full((nodes, lanes), -2, jnp.int32)
    for n in range(nodes):
        par_col = jnp.where(sub == n, parent_ref[n], par_col)
        par_row = jnp.where(lane == n, parent_ref[n], par_row)
    is_root = par_col < 0
    near = (par_row == sub) | (is_root & (lane < nodes))
    up, down = arms(near, (lane - sub) & (NZ - 1))
    up = jnp.broadcast_to(up, (nodes, lanes))
    down = jnp.broadcast_to(down, (nodes, lanes))

    def one(v):
        return jnp.where(v, 1.0, 0.0)

    order = one(lax.broadcasted_iota(jnp.int32, (nodes, nodes), 0) > lax.broadcasted_iota(jnp.int32, (nodes, nodes), 1))

    def edge(e):
        rising = ((e - sub) & (NZ - 1)) < up
        falling = ((sub - 1 - e) & (NZ - 1)) < down
        used = one(rising | falling)
        rank = dot(order, used)
        slot = lax.broadcasted_iota(jnp.int32, (slots, nodes, lanes), 0).astype(F32)
        place = jnp.where(jnp.abs(slot - rank[None]) < 0.5, used[None], 0.0)
        return one(rising), one(falling), place

    up_in, down_in, place_in = edge(z + NZ - 1)
    up_out, down_out, place_out = edge(z)

    def total(v):
        return jnp.sum(v, axis=1, keepdims=True)

    same = up_in * up_out + down_in * down_out
    for j in range(slots):
        relay[0, j] = total(place_out * (place_in[j] * same)[None])
        relay[1, j] = total(place_in * (place_out[j] * same)[None])
    wants = [one(sub == parent_ref[k * NZ + z]) for k in range(NX)] + [one(is_root)]
    for k in range(NX):
        mine = one(sub == k * NZ + z)
        local[0, k] = total(place_out * (up_out * mine)[None])
        local[1, k] = total(place_in * (down_in * mine)[None])
        for m in range(NX + 1):
            here[k, m] = jnp.sum(wants[m] * mine, axis=0, keepdims=True)
    for d in range(ARM):
        far_up = one(((z - sub) & (NZ - 1)) == d + 1) * up_in
        far_down = one(((sub - z) & (NZ - 1)) == d + 1) * down_out
        for m in range(NX + 1):
            remote[0, d, m] = total(place_in * (far_up * wants[m])[None])
            remote[1, d, m] = total(place_out * (far_down * wants[m])[None])

    for kind in ("send", "recv"):
        rows = carried.at[0 : nodes - 1]
        wait = pltpu.make_async_copy(rows, rows, carry_send if kind == "send" else carry_recv)
        wait.wait()
    carried[me] = crow[0]
    decays = carried[:, 0, :]
    for k in range(NX):
        row = jnp.sum(jnp.where(is_root, 0.0, wants[k] * decays), axis=0, keepdims=True)
        scale[k] = jnp.broadcast_to(row, (lanes, lanes)).T[: scale.shape[1], None, :]
    own_copy.wait()

    def z_copy(way, r):
        to = lax.rem(z + (1 if way == 0 else NZ - 1), NZ)
        return pltpu.make_async_remote_copy(
            src_ref=put.at[way, lax.rem(r, 3)],
            dst_ref=got.at[way, r + LAG],
            send_sem=z_send.at[way, lax.rem(r, 3)],
            recv_sem=z_recv.at[way, r],
            device_id=at(x, to),
            device_id_type=MESH,
        )

    def out_copy(hd, k):
        return pltpu.make_async_remote_copy(
            src_ref=res.at[peer(k), hd],
            dst_ref=both_ref.at[x * part + hd],
            send_sem=out_send.at[hd, k - 1],
            recv_sem=out_recv.at[hd, k - 1],
            device_id=at(peer(k), z),
            device_id_type=MESH,
        )

    def own_out(hd):
        return pltpu.make_async_copy(res.at[x, hd], both_ref.at[x * part + hd], out_own.at[hd])

    def piece(k, chunk, kind):
        rows = pl.ds(pl.multiple_of(lax.rem(chunk, 2) * half, half), half)
        return xin[k, chunk // 2, kind, rows, :]

    last = LAG * ARM

    @pl.loop(0, chunks + last)
    def _(r):
        @pl.when((r >= LAG) & (r < rounds + LAG))
        def _():
            for way in range(2):
                z_copy(way, r - LAG).wait_recv()

        @pl.when((lax.rem(r, 2) == 0) & (r < chunks))
        def _():
            hd = r // 2

            @pl.when(hd + ahead < part)
            def _():
                start_in(hd + ahead)

            for k in range(1, NX):
                in_copy(hd, k).wait_recv()
            summed = scale[0, x * part + hd] * xin[0, hd, 1]
            for k in range(1, NX):
                summed += scale[k, x * part + hd] * xin[k, hd, 1]
            extra[hd] = summed

        @pl.when(r < rounds)
        def _():
            @pl.when(r >= 3)
            def _():
                for way in range(2):
                    z_copy(way, r - 3).wait_send()

            for way in range(2):
                now = jnp.minimum(r, chunks - 1)
                acc = local[way, 0] * piece(0, now, 0)[None]
                for k in range(1, NX):
                    acc += local[way, k] * piece(k, now, 0)[None]
                for d in range(ARM):
                    chunk = jnp.clip(r - LAG * (ARM - 1 - d), 0, chunks - 1)
                    for k in range(NX):
                        acc += remote[1 - way, d, k] * piece(k, chunk, 1)[None]
                    rows = pl.ds(pl.multiple_of(lax.rem(chunk, 2) * half, half), half)
                    acc += remote[1 - way, d, NX] * extra[chunk // 2, rows, :][None]
                for j in range(slots):
                    acc += relay[way, j] * got[way, r, j][None]
                put[way, lax.rem(r, 3)] = acc
                z_copy(way, r).start()

        @pl.when(r >= last)
        def _():
            c = r - last
            hd = c // 2
            rows = pl.ds(pl.multiple_of(lax.rem(c, 2) * half, half), half)
            begin = here[0] * piece(0, c, 0)[None]
            for k in range(1, NX):
                begin += here[k] * piece(k, c, 0)[None]
            for way in range(2):
                for d in range(ARM):
                    for j in range(slots):
                        begin += remote[way, d, :, j] * got[way, c + LAG * (d + 1), j][None]
            end = here[:, NX] * extra[hd, rows, :][None]
            for k in range(NX):
                end += here[:, k] * piece(k, c, 1)[None]
            for way in range(2):
                for j in range(slots):
                    end += local[1 - way, :, j] * got[way, c + LAG * ARM, j][None]
            for k in range(NX):
                res[k, hd, 0, rows, :] = begin[k] + scale[k, x * part + hd] * begin[NX]
                res[k, hd, 1, rows, :] = end[k]

            @pl.when(lax.rem(c, 2) == 1)
            def _():
                for k in range(1, NX):
                    out_copy(hd, k).start()
                own_out(hd).start()

    for way in range(2):
        for r in range(rounds - 3, rounds):
            z_copy(way, r).wait_send()

    @pl.loop(0, part)
    def _(hd):
        for k in range(1, NX):
            in_copy(hd, k).wait_send()
            out_copy(hd, k).wait()
        own_out(hd).wait()


def tree(slots, parent, carry, own):
    heads = own.shape[0]
    part = heads // NX
    half = HEAD_DIM // 2
    rounds = part * 2 + LAG * (ARM - 1)
    dma = pltpu.SemaphoreType.DMA
    return pl.pallas_call(
        functools.partial(tree_kernel, slots),
        in_specs=[pl.BlockSpec(memory_space=pltpu.SMEM), pl.BlockSpec(memory_space=pltpu.VMEM), pl.BlockSpec(memory_space=pl.ANY)],
        out_specs=pl.BlockSpec(memory_space=pl.ANY),
        out_shape=sds(own.shape),
        scratch_shapes=[
            pltpu.VMEM((NX, part, 2, HEAD_DIM, STATE), F32),
            pltpu.VMEM((part, HEAD_DIM, STATE), F32),
            pltpu.VMEM((2, rounds + LAG, slots, half, STATE), F32),
            pltpu.VMEM((2, 3, slots, half, STATE), F32),
            pltpu.VMEM((NX, part, 2, HEAD_DIM, STATE), F32),
            pltpu.VMEM((1, 1, STATE), F32),
            pltpu.VMEM((NX * NZ, 1, STATE), F32),
            pltpu.VMEM((NX, heads, 1, STATE), F32),
            pltpu.VMEM((2, slots, slots, 1, STATE), F32),
            pltpu.VMEM((2, NX, slots, 1, STATE), F32),
            pltpu.VMEM((2, ARM, NX + 1, slots, 1, STATE), F32),
            pltpu.VMEM((NX, NX + 1, 1, STATE), F32),
            dma,
            dma((part, NX - 1)),
            dma((part, NX - 1)),
            dma((2, 3)),
            dma((2, rounds)),
            dma((part, NX - 1)),
            dma((part, NX - 1)),
            dma((part,)),
            dma,
            dma,
        ],
        compiler_params=pltpu.CompilerParams(collective_id=slots, has_side_effects=True, vmem_limit_bytes=56 << 20),
        name=f"tree_{slots}",
    )(parent, carry, own)


FEW = 7
ALL = 13


def busiest(parent):
    nodes = NX * NZ
    i = jnp.arange(nodes, dtype=jnp.int32)
    near = (parent[None, :] == i[:, None]) | (parent < 0)[:, None]
    up, down = arms(near, (i[None, :] - i[:, None]) & (NZ - 1))
    e = jnp.arange(NZ, dtype=jnp.int32)[None, :]
    used = (((e - i[:, None]) & (NZ - 1)) < up) | (((i[:, None] - 1 - e) & (NZ - 1)) < down)
    return jnp.max(jnp.sum(used.astype(jnp.int32), axis=0))


def body(inputs, dt_raw, b_proj, c_proj, a_log, dt_bias, skip, grad_out, parent, children):
    heads = a_log.shape[0]
    groups = b_proj.shape[2] // STATE
    per = heads // BLOCK // groups
    x, dy, raw, b, c = inputs[0], grad_out[0], dt_raw[0], b_proj[0], c_proj[0]
    alog, bias, skips = a_log[:, None], dt_bias[:, None], skip[:, None]
    few = lax.pmax(busiest(parent), "dp") <= FEW
    own, carry, xt, dyt = summaries(x, dy, raw, b, c, alog, bias, per)
    inner = inner_grads(dy, raw, b, c, alog, bias, skips, xt, dyt, per)
    both = lax.cond(few, functools.partial(tree, FEW), functools.partial(tree, ALL), parent, carry, own)
    gx, gdt, gb, gc = final_grads(raw, b, c, alog, bias, xt, dyt, both, inner, per)
    return gx[None], gdt[None], gb[None], gc[None]


def solution(mesh):
    placed = (
        P(("dp", "leaf"), None, "heads"),
        P(("dp", "leaf"), "heads", None),
        P(("dp", "leaf"), None, "heads"),
        P(("dp", "leaf"), None, "heads"),
        P("heads"),
        P("heads"),
        P("heads"),
        P(("dp", "leaf"), None, "heads"),
        P("dp"),
        P("dp", None),
    )
    return jax.shard_map(
        body,
        mesh=mesh,
        in_specs=placed,
        out_specs=(
            P(("dp", "leaf"), None, "heads"),
            P(("dp", "leaf"), "heads", None),
            P(("dp", "leaf"), None, "heads"),
            P(("dp", "leaf"), None, "heads"),
        ),
        check_vma=False,
    )
```

```python
import functools

import jax
import jax.numpy as jnp
from jax import lax
from jax.experimental import pallas as pl
from jax.experimental.pallas import tpu as pltpu
from jax.sharding import PartitionSpec as P

HEAD_DIM = 64
STATE = 128
BLOCK = 8
NX = 4
NZ = 8
ARM = 4
LAG = 3
F32 = jnp.float32
BF16 = jnp.bfloat16

MESH = pl.DeviceIdType.MESH


def dot(a, b, da=1, db=0):
    return lax.dot_general(a, b, (((da,), (db,)), ((), ())), preferred_element_type=F32)


def prefix(rows, ones):
    top = rows.astype(BF16)
    rest = rows - top.astype(F32)
    mid = rest.astype(BF16)
    low = (rest - mid.astype(F32)).astype(BF16)
    return dot(top, ones) + (dot(mid, ones) + dot(low, ones))


def triangle(n, lower):
    r = lax.broadcasted_iota(jnp.int32, (n, n), 0)
    c = lax.broadcasted_iota(jnp.int32, (n, n), 1)
    return jnp.where(r >= c if lower else r <= c, 1.0, 0.0).astype(BF16)


def rates(raw, alog, bias):
    v = raw + bias
    rate = jnp.maximum(v, 0.0) + jnp.log1p(jnp.exp(-jnp.abs(v)))
    cum = prefix(-jnp.exp(alog) * rate, triangle(raw.shape[1], False))
    return rate, cum


def spread(rows, flat):
    h, t = rows.shape
    return (flat.astype(F32).reshape(h, -1, t) * rows[:, None, :]).reshape(flat.shape)


def fold(flat, heads):
    return flat.reshape(heads, -1, flat.shape[1]).sum(axis=1)


def first_kernel(x_ref, dy_ref, raw_ref, b_ref, c_ref, alog_ref, bias_ref, own_ref, carry_ref, xt_ref, dyt_ref, rise_ref, fall_ref):
    rate, cum = rates(raw_ref[...], alog_ref[...], bias_ref[...])
    last = cum[:, -1:]
    tail = jnp.exp(last - cum) * rate
    growth = jnp.exp(cum)
    xt = x_ref[...].T
    dyt = dy_ref[...].T
    xt_ref[...] = xt
    dyt_ref[...] = dyt
    end = dot(spread(tail, xt).astype(BF16), b_ref[...])
    pull = dot(spread(growth, dyt).astype(BF16), c_ref[...])
    own_ref[:, 0] = end.reshape(BLOCK, HEAD_DIM, STATE)
    own_ref[:, 1] = pull.reshape(BLOCK, HEAD_DIM, STATE)
    carry_ref[...] = jnp.broadcast_to(jnp.exp(last), carry_ref.shape)
    rise = cum.T
    fall = jnp.log(rate) - cum
    for i in range(BLOCK // 2):
        rise_ref[i] = rise[:, 2 * i : 2 * i + 2]
        fall_ref[i] = fall[2 * i : 2 * i + 2]


def inner_pair(pair, per, skip_ref, dy_ref, b_ref, c_ref, xt_ref, dyt_ref, rise_ref, fall_ref, dx_ref, row_ref, col_ref, dbt_ref, dct_ref, score, summed):
    t = dy_ref.shape[0]
    half = t // 2
    both = 2 * HEAD_DIM
    group = pl.ds(pl.multiple_of(pair // per * STATE, STATE), STATE)

    @pl.when(lax.rem(pair, per) == 0)
    def _():
        score[...] = dot(c_ref[:, group], b_ref[:, group], 1, 1)
        summed[...] = jnp.zeros_like(summed)

    mine = pl.ds(pl.multiple_of(pair * both, both), both)
    rise = rise_ref[pair]
    fall = fall_ref[pair]
    xpair = xt_ref[mine, :]
    dypair = dyt_ref[mine, :]
    dycols = dy_ref[:, mine]
    causal = lax.broadcasted_iota(jnp.int32, (half, half), 0) >= lax.broadcasted_iota(jnp.int32, (half, half), 1)
    where_x = lax.broadcasted_iota(jnp.int32, (both, t), 0) // HEAD_DIM
    lefts, downs, outs = [], [], []
    for i in range(2):
        xhead = jnp.where(where_x == i, xpair, jnp.zeros_like(xpair))
        dyh = dypair[i * HEAD_DIM : (i + 1) * HEAD_DIM]
        skip = skip_ref[2 * pair + i]
        parts = {}
        for a, b in ((0, 0), (1, 0), (1, 1)):
            rows = slice(a * half, (a + 1) * half)
            cols = slice(b * half, (b + 1) * half)
            gap = rise[rows, i : i + 1] + fall[i : i + 1, cols]
            if a == b:
                gap = jnp.where(causal, gap, -1e30)
            decay = jnp.exp(gap)
            mix = decay * score[rows, cols]
            dmix = dot(dycols[rows], xhead[:, cols])
            summed[rows, cols] += dmix * decay
            parts[a, b] = (mix.astype(BF16), dmix * mix)
        q0, q1, q2 = parts[0, 0][1], parts[1, 0][1], parts[1, 1][1]
        downs.append(
            jnp.concatenate([jnp.sum(q0 + q1, axis=0, keepdims=True), jnp.sum(q2, axis=0, keepdims=True)], axis=1)
        )
        lefts.append(
            jnp.concatenate([jnp.sum(q0, axis=1, keepdims=True), jnp.sum(q1 + q2, axis=1, keepdims=True)], axis=0)
        )
        left = jnp.concatenate([parts[0, 0][0], parts[1, 0][0]], axis=0)
        outs.append(
            jnp.concatenate([dot(dyh, left), dot(dyh[:, half:], parts[1, 1][0])], axis=1) + skip * dyh.astype(F32)
        )
    dx_ref[mine, :] = jnp.concatenate(outs, axis=0)
    col_ref[pair] = jnp.concatenate(downs, axis=0)
    row_ref[pair] = jnp.concatenate(lefts, axis=1).T

    @pl.when(lax.rem(pair, per) == per - 1)
    def _():
        r = lax.broadcasted_iota(jnp.int32, (t, t), 0)
        c = lax.broadcasted_iota(jnp.int32, (t, t), 1)
        low = jnp.where(r >= c, summed[...], 0.0).astype(BF16)
        dbt_ref[group, :] = dot(c_ref[:, group], low, 0, 0)
        dct_ref[group, :] = dot(b_ref[:, group], low, 0, 1)


def last_kernel(per, raw_ref, b_ref, c_ref, alog_ref, bias_ref, xt_ref, dyt_ref, both_ref, dx_ref, row_ref, col_ref, dbt_ref, dct_ref, gx_ref, gdt_ref, gb_ref, gc_ref, sumb, sumc):
    step = pl.program_id(0)
    t = raw_ref.shape[1]

    @pl.when(step % per == 0)
    def _():
        sumb[...] = dbt_ref[...]
        sumc[...] = dct_ref[...]

    v = raw_ref[...] + bias_ref[...]
    rate, cum = rates(raw_ref[...], alog_ref[...], bias_ref[...])
    last = cum[:, -1:]
    growth = jnp.exp(cum)
    tail = jnp.exp(last - cum) * rate
    start = both_ref[:, 0].reshape(BLOCK * HEAD_DIM, STATE)
    grad = both_ref[:, 1].reshape(BLOCK * HEAD_DIM, STATE)
    inner = jnp.sum(fold(start * grad, BLOCK), axis=1, keepdims=True)
    start_low = start.astype(BF16)
    grad_low = grad.astype(BF16)
    xt = xt_ref[...]
    dyt = dyt_ref[...]
    pulled = dot(grad_low, b_ref[...], 1, 1)
    z = fold(xt.astype(F32) * pulled, BLOCK) * tail
    gx_ref[...] = (dx_ref[...] + spread(tail, pulled)).astype(BF16).T
    sumb[...] += dot(grad_low, spread(tail, xt).astype(BF16), 0, 0)
    carried = dot(start_low, c_ref[...], 1, 1)
    g = fold(dyt.astype(F32) * carried, BLOCK) * growth
    sumc[...] += dot(start_low, spread(growth, dyt).astype(BF16), 0, 0)
    col = jnp.concatenate([col_ref[i] for i in range(BLOCK // 2)], axis=0)
    row = jnp.concatenate([row_ref[i] for i in range(BLOCK // 2)], axis=0)
    dcum = row - col + g - z
    at_end = jnp.sum(z, axis=1, keepdims=True) + growth[:, -1:] * inner
    dlog = prefix(dcum, triangle(t, True)) + at_end
    slope = 1.0 / (1.0 + jnp.exp(-v))
    gdt_ref[...] = ((col + z) / rate - jnp.exp(alog_ref[...]) * dlog) * slope

    @pl.when(step % per == per - 1)
    def _():
        gb_ref[...] = sumb[...].T
        gc_ref[...] = sumc[...].T


def specs(per, t):
    flat = pl.BlockSpec((BLOCK * HEAD_DIM, t), lambda i: (i, 0))
    return {
        "nat": pl.BlockSpec((t, BLOCK * HEAD_DIM), lambda i: (0, i)),
        "rows": pl.BlockSpec((BLOCK, t), lambda i: (i, 0)),
        "group": pl.BlockSpec((t, STATE), lambda i: (0, i // per)),
        "one": pl.BlockSpec((BLOCK, 1), lambda i: (i, 0)),
        "flat": flat,
        "state": pl.BlockSpec((BLOCK, 2, HEAD_DIM, STATE), lambda i: (i, 0, 0, 0)),
        "lane": pl.BlockSpec((BLOCK, STATE), lambda i: (i, 0)),
        "rise": pl.BlockSpec((BLOCK // 2, t, 2), lambda i: (i, 0, 0)),
        "pairs": pl.BlockSpec((BLOCK // 2, 2, t), lambda i: (i, 0, 0)),
        "groupt": pl.BlockSpec((STATE, t), lambda i: (i // per, 0)),
    }


def params(mib):
    return pltpu.CompilerParams(vmem_limit_bytes=mib << 20)


def sds(shape, kind=F32):
    return jax.ShapeDtypeStruct(shape, kind)


def summaries(x, dy, raw, b, c, alog, bias, per):
    heads, t = raw.shape
    s = specs(per, t)
    return pl.pallas_call(
        first_kernel,
        grid=(heads // BLOCK,),
        in_specs=[s["nat"], s["nat"], s["rows"], s["group"], s["group"], s["one"], s["one"]],
        out_specs=[s["state"], s["lane"], s["flat"], s["flat"], s["rise"], s["pairs"]],
        out_shape=[
            sds((heads, 2, HEAD_DIM, STATE)),
            sds((heads, STATE)),
            sds((heads * HEAD_DIM, t), BF16),
            sds((heads * HEAD_DIM, t), BF16),
            sds((heads // 2, t, 2)),
            sds((heads // 2, 2, t)),
        ],
        compiler_params=params(60),
        name="summaries",
    )(x, dy, raw, b, c, alog, bias)


def final_grads(raw, b, c, alog, bias, xt, dyt, both, inner, per):
    heads, t = raw.shape
    s = specs(per, t)
    groups = heads // BLOCK // per
    return pl.pallas_call(
        functools.partial(last_kernel, per),
        grid=(heads // BLOCK,),
        in_specs=[s["rows"], s["group"], s["group"], s["one"], s["one"], s["flat"], s["flat"], s["state"], s["flat"], s["pairs"], s["pairs"], s["groupt"], s["groupt"]],
        out_specs=[s["nat"], s["rows"], s["group"], s["group"]],
        out_shape=[
            sds((t, heads * HEAD_DIM), BF16),
            sds((heads, t)),
            sds((t, groups * STATE)),
            sds((t, groups * STATE)),
        ],
        scratch_shapes=[pltpu.VMEM((STATE, t), F32), pltpu.VMEM((STATE, t), F32)],
        compiler_params=params(60),
        name="final_grads",
    )(raw, b, c, alog, bias, xt, dyt, both, *inner)


def arms(near, pick):
    def furthest(v):
        return jnp.max(jnp.where(near, v, 0), axis=1, keepdims=True)

    up = furthest(jnp.where(pick < ARM, pick, 0))
    down = furthest(jnp.where(pick > ARM, NZ - pick, 0))
    both = furthest(jnp.where(pick == ARM, 1, 0)) > 0
    return jnp.where(both & (up >= down), ARM, up), jnp.where(both & (up < down), ARM, down)


def tree_kernel(slots, dps, per, parent_ref, carry_ref, own_ref, *refs):
    ins, refs = (refs[:8], refs[8:]) if per else ((), refs)
    (both_ref, most_ref), refs = refs[:2], refs[2:]
    outs, refs = (refs[:5], refs[5:]) if per else ((), refs)
    tree_steps(slots, dps, per, parent_ref, carry_ref, own_ref, ins, both_ref, most_ref, outs, refs[25:], *refs[:25])


def tree_steps(slots, dps, per, parent_ref, carry_ref, own_ref, ins, both_ref, most_ref, outs, temps, counts, count_send, count_recv, xin, extra, got, put, res, crow, carried, scale, relay, local, remote, here,
                own_sem, in_send, in_recv, z_send, z_recv, out_send, out_recv, out_own, carry_send, carry_recv):
    nodes = NX * NZ
    part = own_ref.shape[0] // NX
    half = HEAD_DIM // 2
    chunks = part * 2
    rounds = chunks + LAG * (ARM - 1)
    ahead = 3
    me = lax.axis_index("leaf")
    x, z = me // NZ, lax.rem(me, NZ)

    def peer(k):
        return lax.rem(x + k, NX)

    def at(px, pz):
        return {"leaf": px * NZ + pz}

    barrier = pltpu.get_barrier_semaphore()
    tree_at = lax.axis_index("dp")
    for k in range(1, dps):
        pl.semaphore_signal(barrier, inc=1, device_id={"dp": lax.rem(tree_at + k, dps)}, device_id_type=MESH)

    @pl.loop(1, nodes)
    def _(k):
        pl.semaphore_signal(barrier, inc=1, device_id={"leaf": lax.rem(me + k, nodes)}, device_id_type=MESH)

    crow[...] = jnp.zeros_like(crow)
    crow[0, :, : carry_ref.shape[0]] = carry_ref[...].T[0:1, :]
    got[:, 0:LAG] = jnp.zeros((2, LAG) + got.shape[2:], F32)
    pl.semaphore_wait(barrier, nodes + dps - 2)

    def in_copy(hd, k):
        return pltpu.make_async_remote_copy(
            src_ref=own_ref.at[peer(k) * part + hd],
            dst_ref=xin.at[x, hd],
            send_sem=in_send.at[hd, k - 1],
            recv_sem=in_recv.at[hd, k - 1],
            device_id=at(peer(k), z),
            device_id_type=MESH,
        )

    def start_in(hd):
        for k in range(1, NX):
            in_copy(hd, k).start()

    own_copy = pltpu.make_async_copy(own_ref.at[pl.ds(x * part, part)], xin.at[x], own_sem)
    own_copy.start()
    start_in(0)

    def carry_copy(k):
        return pltpu.make_async_remote_copy(
            src_ref=crow.at[0],
            dst_ref=carried.at[me],
            send_sem=carry_send,
            recv_sem=carry_recv,
            device_id={"leaf": lax.rem(me + k, nodes)},
            device_id_type=MESH,
        )

    @pl.loop(1, nodes)
    def _(k):
        carry_copy(k).start()

    for hd in range(1, ahead):
        start_in(hd)

    lanes = 128
    sub = lax.broadcasted_iota(jnp.int32, (nodes, lanes), 0)
    lane = lax.broadcasted_iota(jnp.int32, (nodes, lanes), 1)
    par_col = jnp.full((nodes, lanes), -1, jnp.int32)
    par_row = jnp.full((nodes, lanes), -2, jnp.int32)
    for n in range(nodes):
        par_col = jnp.where(sub == n, parent_ref[n], par_col)
        par_row = jnp.where(lane == n, parent_ref[n], par_row)
    is_root = par_col < 0
    near = (par_row == sub) | (is_root & (lane < nodes))
    up, down = arms(near, (lane - sub) & (NZ - 1))
    up = jnp.broadcast_to(up, (nodes, lanes))
    down = jnp.broadcast_to(down, (nodes, lanes))

    def one(v):
        return jnp.where(v, 1.0, 0.0)

    order = one(lax.broadcasted_iota(jnp.int32, (nodes, nodes), 0) > lax.broadcasted_iota(jnp.int32, (nodes, nodes), 1))

    def users(e):
        return ((e - sub) & (NZ - 1)) < up, ((sub - 1 - e) & (NZ - 1)) < down

    def used_by(e):
        rising, falling = users(e)
        return one(rising | falling)

    def edge(e):
        rising, falling = users(e)
        used = used_by(e)
        rank = dot(order, used)
        slot = lax.broadcasted_iota(jnp.int32, (slots, nodes, lanes), 0).astype(F32)
        place = jnp.where(jnp.abs(slot - rank[None]) < 0.5, used[None], 0.0)
        return one(rising), one(falling), place

    busy = jnp.zeros((1, lanes), F32)
    for e in range(NZ):
        busy = jnp.maximum(busy, jnp.sum(used_by(e), axis=0, keepdims=True))
    counts[tree_at] = busy

    def count_copy(k):
        return pltpu.make_async_remote_copy(
            src_ref=counts.at[tree_at],
            dst_ref=counts.at[tree_at],
            send_sem=count_send.at[k - 1],
            recv_sem=count_recv.at[k - 1],
            device_id={"dp": lax.rem(tree_at + k, dps)},
            device_id_type=MESH,
        )

    for k in range(1, dps):
        count_copy(k).start()

    up_in, down_in, place_in = edge(z + NZ - 1)
    up_out, down_out, place_out = edge(z)

    def total(v):
        return jnp.sum(v, axis=1, keepdims=True)

    same = up_in * up_out + down_in * down_out
    for j in range(slots):
        relay[0, j] = total(place_out * (place_in[j] * same)[None])
        relay[1, j] = total(place_in * (place_out[j] * same)[None])
    wants = [one(sub == parent_ref[k * NZ + z]) for k in range(NX)] + [one(is_root)]
    for k in range(NX):
        mine = one(sub == k * NZ + z)
        local[0, k] = total(place_out * (up_out * mine)[None])
        local[1, k] = total(place_in * (down_in * mine)[None])
        for m in range(NX + 1):
            here[k, m] = jnp.sum(wants[m] * mine, axis=0, keepdims=True)
    for d in range(ARM):
        far_up = one(((z - sub) & (NZ - 1)) == d + 1) * up_in
        far_down = one(((sub - z) & (NZ - 1)) == d + 1) * down_out
        for m in range(NX + 1):
            remote[0, d, m] = total(place_in * (far_up * wants[m])[None])
            remote[1, d, m] = total(place_out * (far_down * wants[m])[None])

    for kind in ("send", "recv"):
        rows = carried.at[0 : nodes - 1]
        wait = pltpu.make_async_copy(rows, rows, carry_send if kind == "send" else carry_recv)
        wait.wait()
    carried[me] = crow[0]
    decays = carried[:, 0, :]
    for k in range(NX):
        row = jnp.sum(jnp.where(is_root, 0.0, wants[k] * decays), axis=0, keepdims=True)
        scale[k] = jnp.broadcast_to(row, (lanes, lanes)).T[: scale.shape[1], None, :]
    own_copy.wait()

    def z_copy(way, r):
        to = lax.rem(z + (1 if way == 0 else NZ - 1), NZ)
        return pltpu.make_async_remote_copy(
            src_ref=put.at[way, lax.rem(r, 3)],
            dst_ref=got.at[way, r + LAG],
            send_sem=z_send.at[way, lax.rem(r, 3)],
            recv_sem=z_recv.at[way, r],
            device_id=at(x, to),
            device_id_type=MESH,
        )

    def out_copy(hd, k):
        return pltpu.make_async_remote_copy(
            src_ref=res.at[peer(k), hd],
            dst_ref=both_ref.at[x * part + hd],
            send_sem=out_send.at[hd, k - 1],
            recv_sem=out_recv.at[hd, k - 1],
            device_id=at(peer(k), z),
            device_id_type=MESH,
        )

    def own_out(hd):
        return pltpu.make_async_copy(res.at[x, hd], both_ref.at[x * part + hd], out_own.at[hd])

    def piece(k, chunk, kind):
        rows = pl.ds(pl.multiple_of(lax.rem(chunk, 2) * half, half), half)
        return xin[k, chunk // 2, kind, rows, :]

    last = LAG * ARM

    @pl.loop(0, chunks + last)
    def _(r):
        @pl.when((r >= LAG) & (r < rounds + LAG))
        def _():
            for way in range(2):
                z_copy(way, r - LAG).wait_recv()

        @pl.when((lax.rem(r, 2) == 0) & (r < chunks))
        def _():
            hd = r // 2

            @pl.when(hd + ahead < part)
            def _():
                start_in(hd + ahead)

            for k in range(1, NX):
                in_copy(hd, k).wait_recv()
            summed = scale[0, x * part + hd] * xin[0, hd, 1]
            for k in range(1, NX):
                summed += scale[k, x * part + hd] * xin[k, hd, 1]
            extra[hd] = summed

        @pl.when(r < rounds)
        def _():
            @pl.when(r >= 3)
            def _():
                for way in range(2):
                    z_copy(way, r - 3).wait_send()

            for way in range(2):
                now = jnp.minimum(r, chunks - 1)
                acc = local[way, 0] * piece(0, now, 0)[None]
                for k in range(1, NX):
                    acc += local[way, k] * piece(k, now, 0)[None]
                for d in range(ARM):
                    chunk = jnp.clip(r - LAG * (ARM - 1 - d), 0, chunks - 1)
                    for k in range(NX):
                        acc += remote[1 - way, d, k] * piece(k, chunk, 1)[None]
                    rows = pl.ds(pl.multiple_of(lax.rem(chunk, 2) * half, half), half)
                    acc += remote[1 - way, d, NX] * extra[chunk // 2, rows, :][None]
                for j in range(slots):
                    acc += relay[way, j] * got[way, r, j][None]
                put[way, lax.rem(r, 3)] = acc
                z_copy(way, r).start()

        @pl.when(r >= last)
        def _():
            c = r - last
            hd = c // 2
            rows = pl.ds(pl.multiple_of(lax.rem(c, 2) * half, half), half)
            begin = here[0] * piece(0, c, 0)[None]
            for k in range(1, NX):
                begin += here[k] * piece(k, c, 0)[None]
            for way in range(2):
                for d in range(ARM):
                    for j in range(slots):
                        begin += remote[way, d, :, j] * got[way, c + LAG * (d + 1), j][None]
            end = here[:, NX] * extra[hd, rows, :][None]
            for k in range(NX):
                end += here[:, k] * piece(k, c, 1)[None]
            for way in range(2):
                for j in range(slots):
                    end += local[1 - way, :, j] * got[way, c + LAG * ARM, j][None]
            for k in range(NX):
                res[k, hd, 0, rows, :] = begin[k] + scale[k, x * part + hd] * begin[NX]
                res[k, hd, 1, rows, :] = end[k]

            @pl.when(lax.rem(c, 2) == 1)
            def _():
                for k in range(1, NX):
                    out_copy(hd, k).start()
                own_out(hd).start()

        if per:

            @pl.when(r < ins[0].shape[0] // 2)
            def _():
                inner_pair(r, per, *ins, *outs, *temps)

    for k in range(1, dps):
        count_copy(k).wait()
    most = counts[0]
    for k in range(1, dps):
        most = jnp.maximum(most, counts[k])
    most_ref[...] = jnp.broadcast_to(most, most_ref.shape)
    for way in range(2):
        for r in range(rounds - 3, rounds):
            z_copy(way, r).wait_send()

    @pl.loop(0, part)
    def _(hd):
        for k in range(1, NX):
            in_copy(hd, k).wait_send()
            out_copy(hd, k).wait()
        own_out(hd).wait()


def tree(slots, dps, parent, carry, own, inner=()):
    heads = own.shape[0]
    part = heads // NX
    half = HEAD_DIM // 2
    rounds = part * 2 + LAG * (ARM - 1)
    dma = pltpu.SemaphoreType.DMA
    vmem = pl.BlockSpec(memory_space=pltpu.VMEM)
    outs, temps, per = [], [], 0
    if inner:
        t, groups = inner[1].shape[0], inner[2].shape[1] // STATE
        per = heads // 2 // groups
        outs = [
            sds((heads * HEAD_DIM, t)),
            sds((heads // 2, 2, t)),
            sds((heads // 2, 2, t)),
            sds((groups * STATE, t)),
            sds((groups * STATE, t)),
        ]
        temps = [pltpu.VMEM((t, t), F32), pltpu.VMEM((t, t), F32)]
    return pl.pallas_call(
        functools.partial(tree_kernel, slots, dps, per),
        in_specs=[pl.BlockSpec(memory_space=pltpu.SMEM), vmem, pl.BlockSpec(memory_space=pl.ANY)]
        + ([pl.BlockSpec(memory_space=pltpu.SMEM)] + [vmem] * 7 if inner else []),
        out_specs=[pl.BlockSpec(memory_space=pl.ANY), vmem] + [vmem] * len(outs),
        out_shape=[sds(own.shape), sds((8, STATE))] + outs,
        scratch_shapes=[
            pltpu.VMEM((dps, 1, STATE), F32),
            dma((dps,)),
            dma((dps,)),
            pltpu.VMEM((NX, part, 2, HEAD_DIM, STATE), F32),
            pltpu.VMEM((part, HEAD_DIM, STATE), F32),
            pltpu.VMEM((2, rounds + LAG, slots, half, STATE), F32),
            pltpu.VMEM((2, 3, slots, half, STATE), F32),
            pltpu.VMEM((NX, part, 2, HEAD_DIM, STATE), F32),
            pltpu.VMEM((1, 1, STATE), F32),
            pltpu.VMEM((NX * NZ, 1, STATE), F32),
            pltpu.VMEM((NX, heads, 1, STATE), F32),
            pltpu.VMEM((2, slots, slots, 1, STATE), F32),
            pltpu.VMEM((2, NX, slots, 1, STATE), F32),
            pltpu.VMEM((2, ARM, NX + 1, slots, 1, STATE), F32),
            pltpu.VMEM((NX, NX + 1, 1, STATE), F32),
            dma,
            dma((part, NX - 1)),
            dma((part, NX - 1)),
            dma((2, 3)),
            dma((2, rounds)),
            dma((part, NX - 1)),
            dma((part, NX - 1)),
            dma((part,)),
            dma,
            dma,
        ]
        + temps,
        compiler_params=pltpu.CompilerParams(collective_id=slots, has_side_effects=True, vmem_limit_bytes=60 << 20),
        name=f"tree_{slots}",
    )(parent, carry, own, *inner)


FEW = 7
ALL = 13


def body(inputs, dt_raw, b_proj, c_proj, a_log, dt_bias, skip, grad_out, parent, children):
    heads = a_log.shape[0]
    groups = b_proj.shape[2] // STATE
    per = heads // BLOCK // groups
    dps = lax.axis_size("dp")
    x, dy, raw, b, c = inputs[0], grad_out[0], dt_raw[0], b_proj[0], c_proj[0]
    alog, bias = a_log[:, None], dt_bias[:, None]
    own, carry, xt, dyt, rise, fall = summaries(x, dy, raw, b, c, alog, bias, per)
    both, most, *inner = tree(FEW, dps, parent, carry, own, (skip, dy, b, c, xt, dyt, rise, fall))

    def ending(states):
        return final_grads(raw, b, c, alog, bias, xt, dyt, states, inner, per)

    gx, gdt, gb, gc = lax.cond(
        most[0, 0] < FEW + 0.5,
        lambda: tuple(ending(both)),
        lambda: tuple(ending(tree(ALL, dps, parent, carry, own)[0])),
    )
    return gx[None], gdt[None], gb[None], gc[None]


def solution(mesh):
    placed = (
        P(("dp", "leaf"), None, "heads"),
        P(("dp", "leaf"), "heads", None),
        P(("dp", "leaf"), None, "heads"),
        P(("dp", "leaf"), None, "heads"),
        P("heads"),
        P("heads"),
        P("heads"),
        P(("dp", "leaf"), None, "heads"),
        P("dp"),
        P("dp", None),
    )
    return jax.shard_map(
        body,
        mesh=mesh,
        in_specs=placed,
        out_specs=(
            P(("dp", "leaf"), None, "heads"),
            P(("dp", "leaf"), "heads", None),
            P(("dp", "leaf"), None, "heads"),
            P(("dp", "leaf"), None, "heads"),
        ),
        check_vma=False,
    )
```

```python
import functools

import jax
import jax.numpy as jnp
from jax import lax
from jax.experimental import pallas as pl
from jax.experimental.pallas import tpu as pltpu
from jax.sharding import PartitionSpec as P

HEAD_DIM = 64
STATE = 128
NX = 4
NZ = 8
ARM = 4
LAG = 3
F32 = jnp.float32
BF16 = jnp.bfloat16

MESH = pl.DeviceIdType.MESH


def dot(a, b, da=1, db=0):
    return lax.dot_general(a, b, (((da,), (db,)), ((), ())), preferred_element_type=F32)


def prefix(rows, ones):
    top = rows.astype(BF16)
    rest = rows - top.astype(F32)
    mid = rest.astype(BF16)
    low = (rest - mid.astype(F32)).astype(BF16)
    return dot(top, ones) + (dot(mid, ones) + dot(low, ones))


def triangle(n, lower):
    r = lax.broadcasted_iota(jnp.int32, (n, n), 0)
    c = lax.broadcasted_iota(jnp.int32, (n, n), 1)
    return jnp.where(r >= c if lower else r <= c, 1.0, 0.0).astype(BF16)


def spread(rows, flat):
    h, t = rows.shape
    return (flat.astype(F32).reshape(h, -1, t) * rows[:, None, :]).reshape(flat.shape)


def fold(flat, heads):
    return flat.reshape(heads, -1, flat.shape[1]).sum(axis=1)


def scalars(ref, shape):
    row = lax.broadcasted_iota(jnp.int32, shape, 0)
    out = jnp.zeros(shape, F32)
    for h in range(shape[0]):
        out = jnp.where(row == h, ref[h], out)
    return out[:, :1]


def prepare(slots, alog_ref, bias_ref, raw_ref, b_ref, c_ref, rate_s, slope_s, rise_s, fall_s, tail_s, growth_s, ones_s, score, summed, sumb, sumc):
    heads, t = raw_ref.shape
    v = raw_ref[...] + scalars(bias_ref, (heads, STATE))
    rate = jnp.maximum(v, 0.0) + jnp.log1p(jnp.exp(-jnp.abs(v)))
    rate_s[...] = rate
    slope_s[...] = 1.0 / (1.0 + jnp.exp(-v))
    cum = prefix(-jnp.exp(scalars(alog_ref, (heads, STATE))) * rate, triangle(t, False))
    ones_s[...] = triangle(t, True)
    rise = cum.T
    fall = jnp.log(rate) - cum
    tail = jnp.exp(cum[:, -1:] - cum) * rate
    growth = jnp.exp(cum)
    for i in range(heads // 2):
        two = slice(2 * i, 2 * i + 2)
        rise_s[i] = rise[:, two]
        fall_s[i] = fall[two]
        tail_s[i] = tail[two]
        growth_s[i] = growth[two]
    for g in range(score.shape[0]):
        group = slice(g * STATE, (g + 1) * STATE)
        score[g] = dot(c_ref[:, group], b_ref[:, group], 1, 1)
    summed[...] = jnp.zeros_like(summed)
    sumb[...] = jnp.zeros_like(sumb)
    sumc[...] = jnp.zeros_like(sumc)
    return jnp.exp(rise[t - 1 :, :])


def columns(index, width):
    return pl.ds(pl.multiple_of(index * width, width), width)


def summary_pair(pair, group, x_ref, dy_ref, b_ref, c_ref, xt_s, dyt_s, tail_s, growth_s):
    mine = columns(pair, 2 * HEAD_DIM)
    xt = x_ref[:, mine].T
    dyt = dy_ref[:, mine].T
    xt_s[pair] = xt
    dyt_s[pair] = dyt
    end = dot(spread(tail_s[pair], xt).astype(BF16), b_ref[:, columns(group, STATE)])
    pull = dot(spread(growth_s[pair], dyt).astype(BF16), c_ref[:, columns(group, STATE)])
    return end.reshape(2, HEAD_DIM, STATE), pull.reshape(2, HEAD_DIM, STATE)


def inner_pair(pair, group, skip_ref, dy_ref, xt_s, dyt_s, rise_s, fall_s, dx_s, row_s, col_s, score, summed):
    t = dy_ref.shape[0]
    half = t // 2
    both = 2 * HEAD_DIM
    rise = rise_s[pair]
    fall = fall_s[pair]
    xpair = xt_s[pair]
    dypair = dyt_s[pair]
    dycols = dy_ref[:, columns(pair, both)]
    causal = lax.broadcasted_iota(jnp.int32, (half, half), 0) >= lax.broadcasted_iota(jnp.int32, (half, half), 1)
    where_x = lax.broadcasted_iota(jnp.int32, (both, t), 0) // HEAD_DIM
    lefts, downs, outs = [], [], []
    for i in range(2):
        xhead = jnp.where(where_x == i, xpair, jnp.zeros_like(xpair))
        dyh = dypair[i * HEAD_DIM : (i + 1) * HEAD_DIM]
        skip = skip_ref[2 * pair + i]
        parts = {}
        for a, b in ((0, 0), (1, 0), (1, 1)):
            rows = slice(a * half, (a + 1) * half)
            cols = slice(b * half, (b + 1) * half)
            gap = rise[rows, i : i + 1] + fall[i : i + 1, cols]
            if a == b:
                gap = jnp.where(causal, gap, -1e30)
            decay = jnp.exp(gap)
            mix = decay * score[group, rows, cols]
            dmix = dot(dycols[rows], xhead[:, cols])
            summed[group, rows, cols] += dmix * decay
            parts[a, b] = (mix.astype(BF16), dmix * mix)
        q0, q1, q2 = parts[0, 0][1], parts[1, 0][1], parts[1, 1][1]
        downs.append(
            jnp.concatenate([jnp.sum(q0 + q1, axis=0, keepdims=True), jnp.sum(q2, axis=0, keepdims=True)], axis=1)
        )
        lefts.append(
            jnp.concatenate([jnp.sum(q0, axis=1, keepdims=True), jnp.sum(q1 + q2, axis=1, keepdims=True)], axis=0)
        )
        left = jnp.concatenate([parts[0, 0][0], parts[1, 0][0]], axis=0)
        outs.append(
            jnp.concatenate([dot(dyh, left), dot(dyh[:, half:], parts[1, 1][0])], axis=1) + skip * dyh.astype(F32)
        )
    dx_s[pair] = jnp.concatenate(outs, axis=0)
    col_s[pair] = jnp.concatenate(downs, axis=0)
    row_s[pair] = jnp.concatenate(lefts, axis=1).T


def final_pair(pair, group, b_ref, c_ref, states, xt_s, dyt_s, tail_s, growth_s, dx_s, row_s, col_s, sumb, sumc, gx_ref):
    two = pl.ds(2 * pair, 2)
    start = states[two, 0].reshape(2 * HEAD_DIM, STATE)
    grad = states[two, 1].reshape(2 * HEAD_DIM, STATE)
    tail = tail_s[pair]
    growth = growth_s[pair]
    inner = jnp.sum(fold(start * grad, 2), axis=1, keepdims=True)
    start_low = start.astype(BF16)
    grad_low = grad.astype(BF16)
    xt = xt_s[pair]
    dyt = dyt_s[pair]
    own = columns(group, STATE)
    pulled = dot(grad_low, b_ref[:, own], 1, 1)
    z = fold(xt.astype(F32) * pulled, 2) * tail
    gx_ref[:, columns(pair, 2 * HEAD_DIM)] = (dx_s[pair] + spread(tail, pulled)).astype(BF16).T
    sumb[group] += dot(grad_low, spread(tail, xt).astype(BF16), 0, 0)
    carried = dot(start_low, c_ref[:, own], 1, 1)
    g = fold(dyt.astype(F32) * carried, 2) * growth
    sumc[group] += dot(start_low, spread(growth, dyt).astype(BF16), 0, 0)
    col = col_s[pair]
    at_end = jnp.sum(z, axis=1, keepdims=True) + growth[:, -1:] * inner
    lane = lax.broadcasted_iota(jnp.int32, z.shape, 1)
    row_s[pair] = row_s[pair] - col + g - z + jnp.where(lane == z.shape[1] - 1, at_end, 0.0)
    col_s[pair] = col + z


def finish(alog_ref, b_ref, c_ref, rate_s, slope_s, ones_s, row_s, col_s, summed, sumb, sumc, gdt_ref, gb_ref, gc_ref):
    heads, t = rate_s.shape
    dcum = jnp.concatenate([row_s[i] for i in range(heads // 2)], axis=0)
    dlog_rate = jnp.concatenate([col_s[i] for i in range(heads // 2)], axis=0)
    dlog = prefix(dcum, ones_s[...])
    gdt_ref[...] = (dlog_rate / rate_s[...] - jnp.exp(scalars(alog_ref, (heads, STATE))) * dlog) * slope_s[...]
    r = lax.broadcasted_iota(jnp.int32, (t, t), 0)
    c = lax.broadcasted_iota(jnp.int32, (t, t), 1)
    for g in range(summed.shape[0]):
        group = slice(g * STATE, (g + 1) * STATE)
        low = jnp.where(r >= c, summed[g], 0.0).astype(BF16)
        gb_ref[:, group] = (sumb[g] + dot(c_ref[:, group], low, 0, 0)).T
        gc_ref[:, group] = (sumc[g] + dot(b_ref[:, group], low, 0, 1)).T


def arms(near, pick):
    def furthest(v):
        return jnp.max(jnp.where(near, v, 0), axis=1, keepdims=True)

    up = furthest(jnp.where(pick < ARM, pick, 0))
    down = furthest(jnp.where(pick > ARM, NZ - pick, 0))
    both = furthest(jnp.where(pick == ARM, 1, 0)) > 0
    return jnp.where(both & (up >= down), ARM, up), jnp.where(both & (up < down), ARM, down)


def whole_kernel(slots, dps, parent_ref, alog_ref, bias_ref, skip_ref, x_ref, dy_ref, raw_ref, b_ref, c_ref,
                 gx_ref, gdt_ref, gb_ref, gc_ref, most_ref,
                 rate_s, slope_s, rise_s, fall_s, tail_s, growth_s, ones_s, score, summed, sumb, sumc, xt_s, dyt_s, dx_s, row_s, col_s, own_ref, both_ref,
                 counts, count_send, count_recv, xin, extra, got, put, res, crow, carried, scale, relay, local, remote, here,
                 in_send, in_recv, z_send, z_recv, out_send, out_recv, out_own, carry_send, carry_recv):
    nodes = NX * NZ
    part = own_ref.shape[0] // NX
    half = HEAD_DIM // 2
    chunks = part * 2
    rounds = chunks + LAG * (ARM - 1)
    pairs = own_ref.shape[0] // 2
    groups = score.shape[0]
    first = 2 * NX
    me = lax.axis_index("leaf")
    x, z = me // NZ, lax.rem(me, NZ)

    def peer(k):
        return lax.rem(x + k, NX)

    def at(px, pz):
        return {"leaf": px * NZ + pz}

    barrier = pltpu.get_barrier_semaphore()
    tree_at = lax.axis_index("dp")
    for k in range(1, dps):
        pl.semaphore_signal(barrier, inc=1, device_id={"dp": lax.rem(tree_at + k, dps)}, device_id_type=MESH)

    @pl.loop(1, nodes)
    def _(k):
        pl.semaphore_signal(barrier, inc=1, device_id={"leaf": lax.rem(me + k, nodes)}, device_id_type=MESH)

    crow[...] = jnp.zeros_like(crow)
    crow[0, :, : own_ref.shape[0]] = prepare(
        slots, alog_ref, bias_ref, raw_ref, b_ref, c_ref, rate_s, slope_s, rise_s, fall_s, tail_s, growth_s, ones_s, score, summed, sumb, sumc
    )
    got[:, 0:LAG] = jnp.zeros((2, LAG) + got.shape[2:], F32)

    def place(index):
        side = lax.rem(index, NX)
        pair = side * (pairs // NX) + index // NX
        return pair, side, pair // (pairs // groups)

    def summary(index):
        pair, side, group = place(index)
        end, pull = summary_pair(pair, group, x_ref, dy_ref, b_ref, c_ref, xt_s, dyt_s, tail_s, growth_s)
        own_ref[pl.ds(2 * pair, 2), 0] = end
        own_ref[pl.ds(2 * pair, 2), 1] = pull

        @pl.when(side == x)
        def _():
            hd = pl.ds(2 * (index // NX), 2)
            xin[x, hd, 0] = end
            xin[x, hd, 1] = pull

    @pl.loop(0, first)
    def _(index):
        summary(index)

    pl.semaphore_wait(barrier, nodes + dps - 2)

    def in_copy(hd, k):
        return pltpu.make_async_remote_copy(
            src_ref=own_ref.at[peer(k) * part + hd],
            dst_ref=xin.at[x, hd],
            send_sem=in_send.at[hd, k - 1],
            recv_sem=in_recv.at[hd, k - 1],
            device_id=at(peer(k), z),
            device_id_type=MESH,
        )

    def start_in(hd):
        for k in range(1, NX):
            in_copy(hd, k).start()

    start_in(0)

    def carry_copy(k):
        return pltpu.make_async_remote_copy(
            src_ref=crow.at[0],
            dst_ref=carried.at[me],
            send_sem=carry_send,
            recv_sem=carry_recv,
            device_id={"leaf": lax.rem(me + k, nodes)},
            device_id_type=MESH,
        )

    @pl.loop(1, nodes)
    def _(k):
        carry_copy(k).start()

    for hd in range(1, 2 * first // NX):
        start_in(hd)

    lanes = 128
    sub = lax.broadcasted_iota(jnp.int32, (nodes, lanes), 0)
    lane = lax.broadcasted_iota(jnp.int32, (nodes, lanes), 1)
    par_col = jnp.full((nodes, lanes), -1, jnp.int32)
    par_row = jnp.full((nodes, lanes), -2, jnp.int32)
    for n in range(nodes):
        par_col = jnp.where(sub == n, parent_ref[n], par_col)
        par_row = jnp.where(lane == n, parent_ref[n], par_row)
    is_root = par_col < 0
    near = (par_row == sub) | (is_root & (lane < nodes))
    up, down = arms(near, (lane - sub) & (NZ - 1))
    up = jnp.broadcast_to(up, (nodes, lanes))
    down = jnp.broadcast_to(down, (nodes, lanes))

    def one(v):
        return jnp.where(v, 1.0, 0.0)

    order = one(lax.broadcasted_iota(jnp.int32, (nodes, nodes), 0) > lax.broadcasted_iota(jnp.int32, (nodes, nodes), 1))

    def users(e):
        return ((e - sub) & (NZ - 1)) < up, ((sub - 1 - e) & (NZ - 1)) < down

    def used_by(e):
        rising, falling = users(e)
        return one(rising | falling)

    def edge(e):
        rising, falling = users(e)
        used = used_by(e)
        rank = dot(order, used)
        slot = lax.broadcasted_iota(jnp.int32, (slots, nodes, lanes), 0).astype(F32)
        place = jnp.where(jnp.abs(slot - rank[None]) < 0.5, used[None], 0.0)
        return one(rising), one(falling), place

    busy = jnp.zeros((1, lanes), F32)
    for e in range(NZ):
        busy = jnp.maximum(busy, jnp.sum(used_by(e), axis=0, keepdims=True))
    counts[tree_at] = busy

    def count_copy(k):
        return pltpu.make_async_remote_copy(
            src_ref=counts.at[tree_at],
            dst_ref=counts.at[tree_at],
            send_sem=count_send.at[k - 1],
            recv_sem=count_recv.at[k - 1],
            device_id={"dp": lax.rem(tree_at + k, dps)},
            device_id_type=MESH,
        )

    for k in range(1, dps):
        count_copy(k).start()

    up_in, down_in, place_in = edge(z + NZ - 1)
    up_out, down_out, place_out = edge(z)

    def total(v):
        return jnp.sum(v, axis=1, keepdims=True)

    same = up_in * up_out + down_in * down_out
    for j in range(slots):
        relay[0, j] = total(place_out * (place_in[j] * same)[None])
        relay[1, j] = total(place_in * (place_out[j] * same)[None])
    wants = [one(sub == parent_ref[k * NZ + z]) for k in range(NX)] + [one(is_root)]
    for k in range(NX):
        mine = one(sub == k * NZ + z)
        local[0, k] = total(place_out * (up_out * mine)[None])
        local[1, k] = total(place_in * (down_in * mine)[None])
        for m in range(NX + 1):
            here[k, m] = jnp.sum(wants[m] * mine, axis=0, keepdims=True)
    for d in range(ARM):
        far_up = one(((z - sub) & (NZ - 1)) == d + 1) * up_in
        far_down = one(((sub - z) & (NZ - 1)) == d + 1) * down_out
        for m in range(NX + 1):
            remote[0, d, m] = total(place_in * (far_up * wants[m])[None])
            remote[1, d, m] = total(place_out * (far_down * wants[m])[None])

    for kind in ("send", "recv"):
        rows = carried.at[0 : nodes - 1]
        wait = pltpu.make_async_copy(rows, rows, carry_send if kind == "send" else carry_recv)
        wait.wait()
    carried[me] = crow[0]
    decays = carried[:, 0, :]
    for k in range(NX):
        row = jnp.sum(jnp.where(is_root, 0.0, wants[k] * decays), axis=0, keepdims=True)
        scale[k] = jnp.broadcast_to(row, (lanes, lanes)).T[: scale.shape[1], None, :]
    def z_copy(way, r):
        to = lax.rem(z + (1 if way == 0 else NZ - 1), NZ)
        return pltpu.make_async_remote_copy(
            src_ref=put.at[way, lax.rem(r, 3)],
            dst_ref=got.at[way, r + LAG],
            send_sem=z_send.at[way, lax.rem(r, 3)],
            recv_sem=z_recv.at[way, r],
            device_id=at(x, to),
            device_id_type=MESH,
        )

    def out_copy(hd, k):
        return pltpu.make_async_remote_copy(
            src_ref=res.at[peer(k), hd],
            dst_ref=both_ref.at[x * part + hd],
            send_sem=out_send.at[hd, k - 1],
            recv_sem=out_recv.at[hd, k - 1],
            device_id=at(peer(k), z),
            device_id_type=MESH,
        )

    def own_out(hd):
        return pltpu.make_async_copy(res.at[x, hd], both_ref.at[x * part + hd], out_own.at[hd])

    def piece(k, chunk, kind):
        rows = pl.ds(pl.multiple_of(lax.rem(chunk, 2) * half, half), half)
        return xin[k, chunk // 2, kind, rows, :]

    last = LAG * ARM

    late = last + 2 * NX - 2

    @pl.loop(0, pairs + late)
    def _(r):
        @pl.when((r >= LAG) & (r < rounds + LAG))
        def _():
            for way in range(2):
                z_copy(way, r - LAG).wait_recv()

        @pl.when((lax.rem(r, 2) == 0) & (r < chunks))
        def _():
            hd = r // 2

            for k in range(1, NX):
                in_copy(hd, k).wait_recv()
            summed = scale[0, x * part + hd] * xin[0, hd, 1]
            for k in range(1, NX):
                summed += scale[k, x * part + hd] * xin[k, hd, 1]
            extra[hd] = summed

        @pl.when(r < rounds)
        def _():
            @pl.when(r >= 3)
            def _():
                for way in range(2):
                    z_copy(way, r - 3).wait_send()

            for way in range(2):
                now = jnp.minimum(r, chunks - 1)
                acc = local[way, 0] * piece(0, now, 0)[None]
                for k in range(1, NX):
                    acc += local[way, k] * piece(k, now, 0)[None]
                for d in range(ARM):
                    chunk = jnp.clip(r - LAG * (ARM - 1 - d), 0, chunks - 1)
                    for k in range(NX):
                        acc += remote[1 - way, d, k] * piece(k, chunk, 1)[None]
                    rows = pl.ds(pl.multiple_of(lax.rem(chunk, 2) * half, half), half)
                    acc += remote[1 - way, d, NX] * extra[chunk // 2, rows, :][None]
                for j in range(slots):
                    acc += relay[way, j] * got[way, r, j][None]
                put[way, lax.rem(r, 3)] = acc
                z_copy(way, r).start()

        @pl.when((r >= last) & (r < chunks + last))
        def _():
            c = r - last
            hd = c // 2
            rows = pl.ds(pl.multiple_of(lax.rem(c, 2) * half, half), half)
            begin = here[0] * piece(0, c, 0)[None]
            for k in range(1, NX):
                begin += here[k] * piece(k, c, 0)[None]
            for way in range(2):
                for d in range(ARM):
                    for j in range(slots):
                        begin += remote[way, d, :, j] * got[way, c + LAG * (d + 1), j][None]
            end = here[:, NX] * extra[hd, rows, :][None]
            for k in range(NX):
                end += here[:, k] * piece(k, c, 1)[None]
            for way in range(2):
                for j in range(slots):
                    end += local[1 - way, :, j] * got[way, c + LAG * ARM, j][None]
            for k in range(NX):
                res[k, hd, 0, rows, :] = begin[k] + scale[k, x * part + hd] * begin[NX]
                res[k, hd, 1, rows, :] = end[k]

            @pl.when(lax.rem(c, 2) == 1)
            def _():
                for k in range(1, NX):
                    out_copy(hd, k).start()
                own_out(hd).start()

        @pl.when(r + first < pairs)
        def _():
            summary(r + first)

            @pl.when(lax.rem(r + first, NX) == NX - 1)
            def _():
                start_in(2 * ((r + first) // NX))
                start_in(2 * ((r + first) // NX) + 1)

        @pl.when(r < pairs)
        def _():
            pair, side, group = place(r)
            inner_pair(pair, group, skip_ref, dy_ref, xt_s, dyt_s, rise_s, fall_s, dx_s, row_s, col_s, score, summed)

        @pl.when(r >= late)
        def _():
            index = r - late

            @pl.when(lax.rem(index, NX) == 0)
            def _():
                for one_of in range(2):
                    hd = 2 * (index // NX) + one_of
                    for k in range(1, NX):
                        out_copy(hd, k).wait_recv()
                    own_out(hd).wait()

            pair, side, group = place(index)
            final_pair(pair, group, b_ref, c_ref, both_ref, xt_s, dyt_s, tail_s, growth_s, dx_s, row_s, col_s, sumb, sumc, gx_ref)

    finish(alog_ref, b_ref, c_ref, rate_s, slope_s, ones_s, row_s, col_s, summed, sumb, sumc, gdt_ref, gb_ref, gc_ref)
    for k in range(1, dps):
        count_copy(k).wait()
    most = counts[0]
    for k in range(1, dps):
        most = jnp.maximum(most, counts[k])
    most_ref[...] = jnp.broadcast_to(most, most_ref.shape)
    for way in range(2):
        for r in range(rounds - 3, rounds):
            z_copy(way, r).wait_send()

    @pl.loop(0, part)
    def _(hd):
        for k in range(1, NX):
            in_copy(hd, k).wait_send()
            out_copy(hd, k).wait_send()


def sds(shape, kind=F32):
    return jax.ShapeDtypeStruct(shape, kind)


def whole(slots, dps, parent, alog, bias, skip, x, dy, raw, b, c):
    heads, t = raw.shape
    pairs = heads // 2
    groups = b.shape[1] // STATE
    part = heads // NX
    half = HEAD_DIM // 2
    rounds = part * 2 + LAG * (ARM - 1)
    dma = pltpu.SemaphoreType.DMA
    vmem = pl.BlockSpec(memory_space=pltpu.VMEM)
    smem = pl.BlockSpec(memory_space=pltpu.SMEM)
    rows = pltpu.VMEM((pairs, 2, t), F32)
    turned = pltpu.VMEM((pairs, 2 * HEAD_DIM, t), BF16)
    return pl.pallas_call(
        functools.partial(whole_kernel, slots, dps),
        in_specs=[smem] * 4 + [vmem] * 5,
        out_specs=[vmem] * 5,
        out_shape=[
            sds((t, heads * HEAD_DIM), BF16),
            sds((heads, t)),
            sds((t, groups * STATE)),
            sds((t, groups * STATE)),
            sds((8, STATE)),
        ],
        scratch_shapes=[
            pltpu.VMEM((heads, t), F32),
            pltpu.VMEM((heads, t), F32),
            pltpu.VMEM((pairs, t, 2), F32),
            rows,
            rows,
            rows,
            pltpu.VMEM((t, t), BF16),
            pltpu.VMEM((groups, t, t), F32),
            pltpu.VMEM((groups, t, t), F32),
            pltpu.VMEM((groups, STATE, t), F32),
            pltpu.VMEM((groups, STATE, t), F32),
            turned,
            turned,
            pltpu.VMEM((pairs, 2 * HEAD_DIM, t), F32),
            rows,
            rows,
            pltpu.VMEM((heads, 2, HEAD_DIM, STATE), F32),
            pltpu.VMEM((heads, 2, HEAD_DIM, STATE), F32),
            pltpu.VMEM((dps, 1, STATE), F32),
            dma((dps,)),
            dma((dps,)),
            pltpu.VMEM((NX, part, 2, HEAD_DIM, STATE), F32),
            pltpu.VMEM((part, HEAD_DIM, STATE), F32),
            pltpu.VMEM((2, rounds + LAG, slots, half, STATE), F32),
            pltpu.VMEM((2, 3, slots, half, STATE), F32),
            pltpu.VMEM((NX, part, 2, HEAD_DIM, STATE), F32),
            pltpu.VMEM((1, 1, STATE), F32),
            pltpu.VMEM((NX * NZ, 1, STATE), F32),
            pltpu.VMEM((NX, heads, 1, STATE), F32),
            pltpu.VMEM((2, slots, slots, 1, STATE), F32),
            pltpu.VMEM((2, NX, slots, 1, STATE), F32),
            pltpu.VMEM((2, ARM, NX + 1, slots, 1, STATE), F32),
            pltpu.VMEM((NX, NX + 1, 1, STATE), F32),
            dma((part, NX - 1)),
            dma((part, NX - 1)),
            dma((2, 3)),
            dma((2, rounds)),
            dma((part, NX - 1)),
            dma((part, NX - 1)),
            dma((part,)),
            dma,
            dma,
        ],
        compiler_params=pltpu.CompilerParams(collective_id=slots, has_side_effects=True, vmem_limit_bytes=62 << 20),
        name=f"whole_{slots}",
    )(parent, alog, bias, skip, x, dy, raw, b, c)


FEW = 7
ALL = 13


def body(inputs, dt_raw, b_proj, c_proj, a_log, dt_bias, skip, grad_out, parent, children):
    given = (parent, a_log, dt_bias, skip, inputs[0], grad_out[0], dt_raw[0], b_proj[0], c_proj[0])
    dps = lax.axis_size("dp")
    *grads, most = whole(FEW, dps, *given)
    grads = lax.cond(most[0, 0] < FEW + 0.5, lambda: tuple(grads), lambda: tuple(whole(ALL, dps, *given)[:4]))
    return tuple(g[None] for g in grads)


def solution(mesh):
    placed = (
        P(("dp", "leaf"), None, "heads"),
        P(("dp", "leaf"), "heads", None),
        P(("dp", "leaf"), None, "heads"),
        P(("dp", "leaf"), None, "heads"),
        P("heads"),
        P("heads"),
        P("heads"),
        P(("dp", "leaf"), None, "heads"),
        P("dp"),
        P("dp", None),
    )
    return jax.shard_map(
        body,
        mesh=mesh,
        in_specs=placed,
        out_specs=(
            P(("dp", "leaf"), None, "heads"),
            P(("dp", "leaf"), "heads", None),
            P(("dp", "leaf"), None, "heads"),
            P(("dp", "leaf"), None, "heads"),
        ),
        check_vma=False,
    )
```

```python
import functools

import jax
import jax.numpy as jnp
from jax import lax
from jax.experimental import pallas as pl
from jax.experimental.pallas import tpu as pltpu
from jax.sharding import PartitionSpec as P

HEAD_DIM = 64
STATE = 128
NX = 4
NZ = 8
PIECES = 4
ARM = 5
LAG = 4
F32 = jnp.float32
BF16 = jnp.bfloat16

MESH = pl.DeviceIdType.MESH


def dot(a, b, da=1, db=0):
    return lax.dot_general(a, b, (((da,), (db,)), ((), ())), preferred_element_type=F32)


def prefix(rows, ones):
    top = rows.astype(BF16)
    rest = rows - top.astype(F32)
    mid = rest.astype(BF16)
    low = (rest - mid.astype(F32)).astype(BF16)
    return dot(top, ones) + (dot(mid, ones) + dot(low, ones))


def triangle(n, lower):
    r = lax.broadcasted_iota(jnp.int32, (n, n), 0)
    c = lax.broadcasted_iota(jnp.int32, (n, n), 1)
    return jnp.where(r >= c if lower else r <= c, 1.0, 0.0).astype(BF16)


def spread(rows, flat):
    h, t = rows.shape
    return (flat.astype(F32).reshape(h, -1, t) * rows[:, None, :]).reshape(flat.shape)


def fold(flat, heads):
    return flat.reshape(heads, -1, flat.shape[1]).sum(axis=1)


def scalars(ref, shape):
    row = lax.broadcasted_iota(jnp.int32, shape, 0)
    out = jnp.zeros(shape, F32)
    for h in range(shape[0]):
        out = jnp.where(row == h, ref[h], out)
    return out[:, :1]


def prepare(slots, alog_ref, bias_ref, raw_ref, b_ref, c_ref, rate_s, slope_s, rise_s, fall_s, tail_s, growth_s, ones_s, score, summed, sumb, sumc):
    heads, t = raw_ref.shape
    v = raw_ref[...] + scalars(bias_ref, (heads, STATE))
    rate = jnp.maximum(v, 0.0) + jnp.log1p(jnp.exp(-jnp.abs(v)))
    rate_s[...] = rate
    slope_s[...] = 1.0 / (1.0 + jnp.exp(-v))
    cum = prefix(-jnp.exp(scalars(alog_ref, (heads, STATE))) * rate, triangle(t, False))
    ones_s[...] = triangle(t, True)
    rise = cum.T
    fall = jnp.log(rate) - cum
    tail = jnp.exp(cum[:, -1:] - cum) * rate
    growth = jnp.exp(cum)
    for i in range(heads // 2):
        two = slice(2 * i, 2 * i + 2)
        rise_s[i] = rise[:, two]
        fall_s[i] = fall[two]
        tail_s[i] = tail[two]
        growth_s[i] = growth[two]
    for g in range(score.shape[0]):
        group = slice(g * STATE, (g + 1) * STATE)
        score[g] = dot(c_ref[:, group], b_ref[:, group], 1, 1)
    summed[...] = jnp.zeros_like(summed)
    sumb[...] = jnp.zeros_like(sumb)
    sumc[...] = jnp.zeros_like(sumc)
    return jnp.exp(rise[t - 1 :, :])


def columns(index, width):
    return pl.ds(pl.multiple_of(index * width, width), width)


def summary_pair(pair, group, x_ref, dy_ref, b_ref, c_ref, xt_s, dyt_s, tail_s, growth_s):
    mine = columns(pair, 2 * HEAD_DIM)
    xt = x_ref[:, mine].T
    dyt = dy_ref[:, mine].T
    xt_s[pair] = xt
    dyt_s[pair] = dyt
    end = dot(spread(tail_s[pair], xt).astype(BF16), b_ref[:, columns(group, STATE)])
    pull = dot(spread(growth_s[pair], dyt).astype(BF16), c_ref[:, columns(group, STATE)])
    return end.reshape(2, HEAD_DIM, STATE), pull.reshape(2, HEAD_DIM, STATE)


def inner_pair(pair, group, skip_ref, dy_ref, xt_s, dyt_s, rise_s, fall_s, dx_s, row_s, col_s, score, summed):
    t = dy_ref.shape[0]
    half = t // 2
    both = 2 * HEAD_DIM
    rise = rise_s[pair]
    fall = fall_s[pair]
    xpair = xt_s[pair]
    dypair = dyt_s[pair]
    dycols = dy_ref[:, columns(pair, both)]
    causal = lax.broadcasted_iota(jnp.int32, (half, half), 0) >= lax.broadcasted_iota(jnp.int32, (half, half), 1)
    where_x = lax.broadcasted_iota(jnp.int32, (both, t), 0) // HEAD_DIM
    lefts, downs, outs = [], [], []
    for i in range(2):
        xhead = jnp.where(where_x == i, xpair, jnp.zeros_like(xpair))
        dyh = dypair[i * HEAD_DIM : (i + 1) * HEAD_DIM]
        skip = skip_ref[2 * pair + i]
        parts = {}
        for a, b in ((0, 0), (1, 0), (1, 1)):
            rows = slice(a * half, (a + 1) * half)
            cols = slice(b * half, (b + 1) * half)
            gap = rise[rows, i : i + 1] + fall[i : i + 1, cols]
            if a == b:
                gap = jnp.where(causal, gap, -1e30)
            decay = jnp.exp(gap)
            mix = decay * score[group, rows, cols]
            dmix = dot(dycols[rows], xhead[:, cols])
            summed[group, rows, cols] += dmix * decay
            parts[a, b] = (mix.astype(BF16), dmix * mix)
        q0, q1, q2 = parts[0, 0][1], parts[1, 0][1], parts[1, 1][1]
        downs.append(
            jnp.concatenate([jnp.sum(q0 + q1, axis=0, keepdims=True), jnp.sum(q2, axis=0, keepdims=True)], axis=1)
        )
        lefts.append(
            jnp.concatenate([jnp.sum(q0, axis=1, keepdims=True), jnp.sum(q1 + q2, axis=1, keepdims=True)], axis=0)
        )
        left = jnp.concatenate([parts[0, 0][0], parts[1, 0][0]], axis=0)
        outs.append(
            jnp.concatenate([dot(dyh, left), dot(dyh[:, half:], parts[1, 1][0])], axis=1) + skip * dyh.astype(F32)
        )
    dx_s[pair] = jnp.concatenate(outs, axis=0)
    col_s[pair] = jnp.concatenate(downs, axis=0)
    row_s[pair] = jnp.concatenate(lefts, axis=1).T


def final_pair(pair, group, b_ref, c_ref, states, xt_s, dyt_s, tail_s, growth_s, dx_s, row_s, col_s, sumb, sumc, gx_ref):
    two = pl.ds(2 * pair, 2)
    start = states[two, 0].reshape(2 * HEAD_DIM, STATE)
    grad = states[two, 1].reshape(2 * HEAD_DIM, STATE)
    tail = tail_s[pair]
    growth = growth_s[pair]
    inner = jnp.sum(fold(start * grad, 2), axis=1, keepdims=True)
    start_low = start.astype(BF16)
    grad_low = grad.astype(BF16)
    xt = xt_s[pair]
    dyt = dyt_s[pair]
    own = columns(group, STATE)
    pulled = dot(grad_low, b_ref[:, own], 1, 1)
    z = fold(xt.astype(F32) * pulled, 2) * tail
    gx_ref[:, columns(pair, 2 * HEAD_DIM)] = (dx_s[pair] + spread(tail, pulled)).astype(BF16).T
    sumb[group] += dot(grad_low, spread(tail, xt).astype(BF16), 0, 0)
    carried = dot(start_low, c_ref[:, own], 1, 1)
    g = fold(dyt.astype(F32) * carried, 2) * growth
    sumc[group] += dot(start_low, spread(growth, dyt).astype(BF16), 0, 0)
    col = col_s[pair]
    at_end = jnp.sum(z, axis=1, keepdims=True) + growth[:, -1:] * inner
    lane = lax.broadcasted_iota(jnp.int32, z.shape, 1)
    row_s[pair] = row_s[pair] - col + g - z + jnp.where(lane == z.shape[1] - 1, at_end, 0.0)
    col_s[pair] = col + z


def finish(alog_ref, b_ref, c_ref, rate_s, slope_s, ones_s, row_s, col_s, summed, sumb, sumc, gdt_ref, gb_ref, gc_ref):
    heads, t = rate_s.shape
    dcum = jnp.concatenate([row_s[i] for i in range(heads // 2)], axis=0)
    dlog_rate = jnp.concatenate([col_s[i] for i in range(heads // 2)], axis=0)
    dlog = prefix(dcum, ones_s[...])
    gdt_ref[...] = (dlog_rate / rate_s[...] - jnp.exp(scalars(alog_ref, (heads, STATE))) * dlog) * slope_s[...]
    r = lax.broadcasted_iota(jnp.int32, (t, t), 0)
    c = lax.broadcasted_iota(jnp.int32, (t, t), 1)
    for g in range(summed.shape[0]):
        group = slice(g * STATE, (g + 1) * STATE)
        low = jnp.where(r >= c, summed[g], 0.0).astype(BF16)
        gb_ref[:, group] = (sumb[g] + dot(c_ref[:, group], low, 0, 0)).T
        gc_ref[:, group] = (sumc[g] + dot(b_ref[:, group], low, 0, 1)).T


def arms(near, sub, lane):
    pick = (lane - sub) & (NZ - 1)
    ups, downs, covers = [], [], []
    for k in range(NZ - ARM - 1, ARM + 1):
        up = jnp.max(jnp.where(near & (pick <= k), pick, 0), axis=1, keepdims=True)
        down = jnp.max(jnp.where(near & (pick > k), NZ - pick, 0), axis=1, keepdims=True)
        used = (((lane - sub) & (NZ - 1)) < up) | (((sub - 1 - lane) & (NZ - 1)) < down)
        ups.append(jnp.broadcast_to(up, sub.shape))
        downs.append(jnp.broadcast_to(down, sub.shape))
        covers.append(jnp.where(used & (lane < NZ), 1.0, 0.0))
    up, down, now = ups[0], downs[0], covers[0]
    least = jnp.sum(now, axis=1, keepdims=True)
    for k in range(1, len(covers)):
        steps = jnp.sum(covers[k], axis=1, keepdims=True)
        less = jnp.broadcast_to(steps < least, sub.shape)
        up, down, now = jnp.where(less, ups[k], up), jnp.where(less, downs[k], down), jnp.where(less, covers[k], now)
        least = jnp.minimum(steps, least)
    for _ in range(3):
        load = jnp.sum(now, axis=0, keepdims=True) - now
        costs = []
        for cover in covers:
            cost = jnp.where(lane < NZ, jnp.exp((load + cover) * 1.3862944), 0.0)
            costs.append(jnp.broadcast_to(jnp.sum(cost, axis=1, keepdims=True), sub.shape))
        best = functools.reduce(jnp.minimum, costs)
        best = jnp.min(best, axis=0, keepdims=True)
        names = [jnp.where(cost == best, k * NX * NZ + sub, NX * NZ * NZ) for k, cost in enumerate(costs)]
        name = jnp.min(functools.reduce(jnp.minimum, names), axis=0, keepdims=True)
        for k in range(len(covers)):
            hit = name == k * NX * NZ + sub
            up, down, now = jnp.where(hit, ups[k], up), jnp.where(hit, downs[k], down), jnp.where(hit, covers[k], now)
    return up, down


def whole_kernel(slots, dps, parent_ref, alog_ref, bias_ref, skip_ref, x_ref, dy_ref, raw_ref, b_ref, c_ref,
                 gx_ref, gdt_ref, gb_ref, gc_ref, most_ref,
                 rate_s, slope_s, rise_s, fall_s, tail_s, growth_s, ones_s, score, summed, sumb, sumc, xt_s, dyt_s, dx_s, row_s, col_s, own_ref, both_ref,
                 counts, count_send, count_recv, xin, extra, got, put, res, crow, carried, scale, relay, local, remote, here,
                 in_send, in_recv, z_send, z_recv, out_send, out_recv, out_own, carry_send, carry_recv):
    nodes = NX * NZ
    part = own_ref.shape[0] // NX
    size = HEAD_DIM // PIECES
    chunks = part * PIECES
    rounds = chunks + LAG * (ARM - 1)
    pairs = own_ref.shape[0] // 2
    groups = score.shape[0]
    first = 2 * NX
    me = lax.axis_index("leaf")
    x, z = me // NZ, lax.rem(me, NZ)

    def peer(k):
        return lax.rem(x + k, NX)

    def at(px, pz):
        return {"leaf": px * NZ + pz}

    barrier = pltpu.get_barrier_semaphore()
    tree_at = lax.axis_index("dp")
    for k in range(1, dps):
        pl.semaphore_signal(barrier, inc=1, device_id={"dp": lax.rem(tree_at + k, dps)}, device_id_type=MESH)

    @pl.loop(1, nodes)
    def _(k):
        pl.semaphore_signal(barrier, inc=1, device_id={"leaf": lax.rem(me + k, nodes)}, device_id_type=MESH)

    crow[...] = jnp.zeros_like(crow)
    crow[0, :, : own_ref.shape[0]] = prepare(
        slots, alog_ref, bias_ref, raw_ref, b_ref, c_ref, rate_s, slope_s, rise_s, fall_s, tail_s, growth_s, ones_s, score, summed, sumb, sumc
    )
    got[:, 0:LAG] = jnp.zeros((2, LAG) + got.shape[2:], F32)

    def place(index):
        side = lax.rem(index, NX)
        pair = side * (pairs // NX) + index // NX
        return pair, side, pair // (pairs // groups)

    def summary(index):
        pair, side, group = place(index)
        end, pull = summary_pair(pair, group, x_ref, dy_ref, b_ref, c_ref, xt_s, dyt_s, tail_s, growth_s)
        own_ref[pl.ds(2 * pair, 2), 0] = end
        own_ref[pl.ds(2 * pair, 2), 1] = pull

        @pl.when(side == x)
        def _():
            hd = pl.ds(2 * (index // NX), 2)
            xin[x, hd, 0] = end
            xin[x, hd, 1] = pull

    @pl.loop(0, first)
    def _(index):
        summary(index)

    pl.semaphore_wait(barrier, nodes + dps - 2)

    def in_copy(hd, k):
        return pltpu.make_async_remote_copy(
            src_ref=own_ref.at[peer(k) * part + hd],
            dst_ref=xin.at[x, hd],
            send_sem=in_send.at[hd, k - 1],
            recv_sem=in_recv.at[hd, k - 1],
            device_id=at(peer(k), z),
            device_id_type=MESH,
        )

    def start_in(hd):
        for k in range(1, NX):
            in_copy(hd, k).start()

    start_in(0)

    def carry_copy(k):
        return pltpu.make_async_remote_copy(
            src_ref=crow.at[0],
            dst_ref=carried.at[me],
            send_sem=carry_send,
            recv_sem=carry_recv,
            device_id={"leaf": lax.rem(me + k, nodes)},
            device_id_type=MESH,
        )

    @pl.loop(1, nodes)
    def _(k):
        carry_copy(k).start()

    for hd in range(1, 2 * first // NX):
        start_in(hd)

    lanes = 128
    sub = lax.broadcasted_iota(jnp.int32, (nodes, lanes), 0)
    lane = lax.broadcasted_iota(jnp.int32, (nodes, lanes), 1)
    par_col = jnp.full((nodes, lanes), -1, jnp.int32)
    par_row = jnp.full((nodes, lanes), -2, jnp.int32)
    for n in range(nodes):
        par_col = jnp.where(sub == n, parent_ref[n], par_col)
        par_row = jnp.where(lane == n, parent_ref[n], par_row)
    is_root = par_col < 0
    near = (par_row == sub) | (is_root & (lane < nodes))
    up, down = arms(near, sub, lane)

    def one(v):
        return jnp.where(v, 1.0, 0.0)

    order = one(lax.broadcasted_iota(jnp.int32, (nodes, nodes), 0) > lax.broadcasted_iota(jnp.int32, (nodes, nodes), 1))

    def users(e):
        return ((e - sub) & (NZ - 1)) < up, ((sub - 1 - e) & (NZ - 1)) < down

    def used_by(e):
        rising, falling = users(e)
        return one(rising | falling)

    def edge(e):
        rising, falling = users(e)
        used = used_by(e)
        rank = dot(order, used)
        slot = lax.broadcasted_iota(jnp.int32, (slots, nodes, lanes), 0).astype(F32)
        place = jnp.where(jnp.abs(slot - rank[None]) < 0.5, used[None], 0.0)
        return one(rising), one(falling), place

    busy = jnp.zeros((1, lanes), F32)
    for e in range(NZ):
        busy = jnp.maximum(busy, jnp.sum(used_by(e), axis=0, keepdims=True))
    counts[tree_at] = busy

    def count_copy(k):
        return pltpu.make_async_remote_copy(
            src_ref=counts.at[tree_at],
            dst_ref=counts.at[tree_at],
            send_sem=count_send.at[k - 1],
            recv_sem=count_recv.at[k - 1],
            device_id={"dp": lax.rem(tree_at + k, dps)},
            device_id_type=MESH,
        )

    for k in range(1, dps):
        count_copy(k).start()

    up_in, down_in, place_in = edge(z + NZ - 1)
    up_out, down_out, place_out = edge(z)

    def total(v):
        return jnp.sum(v, axis=1, keepdims=True)

    same = up_in * up_out + down_in * down_out
    for j in range(slots):
        relay[0, j] = total(place_out * (place_in[j] * same)[None])
        relay[1, j] = total(place_in * (place_out[j] * same)[None])
    wants = [one(sub == parent_ref[k * NZ + z]) for k in range(NX)] + [one(is_root)]
    for k in range(NX):
        mine = one(sub == k * NZ + z)
        local[0, k] = total(place_out * (up_out * mine)[None])
        local[1, k] = total(place_in * (down_in * mine)[None])
        for m in range(NX + 1):
            here[k, m] = jnp.sum(wants[m] * mine, axis=0, keepdims=True)
    for d in range(ARM):
        far_up = one(((z - sub) & (NZ - 1)) == d + 1) * up_in
        far_down = one(((sub - z) & (NZ - 1)) == d + 1) * down_out
        for m in range(NX + 1):
            remote[0, d, m] = total(place_in * (far_up * wants[m])[None])
            remote[1, d, m] = total(place_out * (far_down * wants[m])[None])

    for kind in ("send", "recv"):
        rows = carried.at[0 : nodes - 1]
        wait = pltpu.make_async_copy(rows, rows, carry_send if kind == "send" else carry_recv)
        wait.wait()
    carried[me] = crow[0]
    decays = carried[:, 0, :]
    for k in range(NX):
        row = jnp.sum(jnp.where(is_root, 0.0, wants[k] * decays), axis=0, keepdims=True)
        scale[k] = jnp.broadcast_to(row, (lanes, lanes)).T[: scale.shape[1], None, :]
    def z_copy(way, r):
        to = lax.rem(z + (1 if way == 0 else NZ - 1), NZ)
        return pltpu.make_async_remote_copy(
            src_ref=put.at[way, lax.rem(r, 3)],
            dst_ref=got.at[way, r + LAG],
            send_sem=z_send.at[way, lax.rem(r, 3)],
            recv_sem=z_recv.at[way, r],
            device_id=at(x, to),
            device_id_type=MESH,
        )

    def out_copy(hd, k):
        return pltpu.make_async_remote_copy(
            src_ref=res.at[peer(k), hd],
            dst_ref=both_ref.at[x * part + hd],
            send_sem=out_send.at[hd, k - 1],
            recv_sem=out_recv.at[hd, k - 1],
            device_id=at(peer(k), z),
            device_id_type=MESH,
        )

    def own_out(hd):
        return pltpu.make_async_copy(res.at[x, hd], both_ref.at[x * part + hd], out_own.at[hd])

    def part_of(chunk):
        return pl.ds(pl.multiple_of(lax.rem(chunk, PIECES) * size, size), size)

    def piece(k, chunk, kind):
        return xin[k, chunk // PIECES, kind, part_of(chunk), :]

    last = LAG * ARM

    steps = PIECES // 2
    late = last + 2 * PIECES + 3

    @pl.loop(0, steps * (pairs - 1) + late + 1)
    def _(r):
        @pl.when((r >= LAG) & (r < rounds + LAG))
        def _():
            for way in range(2):
                z_copy(way, r - LAG).wait_recv()

        @pl.when((lax.rem(r, PIECES) == 0) & (r < chunks))
        def _():
            hd = r // PIECES

            for k in range(1, NX):
                in_copy(hd, k).wait_recv()
            summed = scale[0, x * part + hd] * xin[0, hd, 1]
            for k in range(1, NX):
                summed += scale[k, x * part + hd] * xin[k, hd, 1]
            extra[hd] = summed

        @pl.when(r < rounds)
        def _():
            @pl.when(r >= 3)
            def _():
                for way in range(2):
                    z_copy(way, r - 3).wait_send()

            for way in range(2):
                now = jnp.minimum(r, chunks - 1)
                acc = local[way, 0] * piece(0, now, 0)[None]
                for k in range(1, NX):
                    acc += local[way, k] * piece(k, now, 0)[None]
                for d in range(ARM):
                    chunk = jnp.clip(r - LAG * (ARM - 1 - d), 0, chunks - 1)
                    for k in range(NX):
                        acc += remote[1 - way, d, k] * piece(k, chunk, 1)[None]
                    acc += remote[1 - way, d, NX] * extra[chunk // PIECES, part_of(chunk), :][None]
                for j in range(slots):
                    acc += relay[way, j] * got[way, r, j][None]
                put[way, lax.rem(r, 3)] = acc
                z_copy(way, r).start()

        @pl.when((r >= last) & (r < chunks + last))
        def _():
            c = r - last
            hd = c // PIECES
            rows = part_of(c)
            begin = here[0] * piece(0, c, 0)[None]
            for k in range(1, NX):
                begin += here[k] * piece(k, c, 0)[None]
            for way in range(2):
                for d in range(ARM):
                    for j in range(slots):
                        begin += remote[way, d, :, j] * got[way, c + LAG * (d + 1), j][None]
            end = here[:, NX] * extra[hd, rows, :][None]
            for k in range(NX):
                end += here[:, k] * piece(k, c, 1)[None]
            for way in range(2):
                for j in range(slots):
                    end += local[1 - way, :, j] * got[way, c + LAG * ARM, j][None]
            for k in range(NX):
                res[k, hd, 0, rows, :] = begin[k] + scale[k, x * part + hd] * begin[NX]
                res[k, hd, 1, rows, :] = end[k]

            @pl.when(lax.rem(c, PIECES) == PIECES - 1)
            def _():
                for k in range(1, NX):
                    out_copy(hd, k).start()
                own_out(hd).start()

        @pl.when((lax.rem(r, steps) == 1) & (r // steps + first < pairs))
        def _():
            index = r // steps + first
            summary(index)

            @pl.when(lax.rem(index, NX) == NX - 1)
            def _():
                start_in(2 * (index // NX))
                start_in(2 * (index // NX) + 1)

        @pl.when((lax.rem(r, steps) == 0) & (r // steps < pairs))
        def _():
            pair, side, group = place(r // steps)
            inner_pair(pair, group, skip_ref, dy_ref, xt_s, dyt_s, rise_s, fall_s, dx_s, row_s, col_s, score, summed)

        @pl.when((r >= late) & (lax.rem(r - late, steps) == 0))
        def _():
            index = (r - late) // steps

            @pl.when(lax.rem(index, NX) == 0)
            def _():
                for one_of in range(2):
                    hd = 2 * (index // NX) + one_of
                    for k in range(1, NX):
                        out_copy(hd, k).wait_recv()
                    own_out(hd).wait()

            pair, side, group = place(index)
            final_pair(pair, group, b_ref, c_ref, both_ref, xt_s, dyt_s, tail_s, growth_s, dx_s, row_s, col_s, sumb, sumc, gx_ref)

    finish(alog_ref, b_ref, c_ref, rate_s, slope_s, ones_s, row_s, col_s, summed, sumb, sumc, gdt_ref, gb_ref, gc_ref)
    for k in range(1, dps):
        count_copy(k).wait()
    most = counts[0]
    for k in range(1, dps):
        most = jnp.maximum(most, counts[k])
    most_ref[...] = jnp.broadcast_to(most, most_ref.shape)
    for way in range(2):
        for r in range(rounds - 3, rounds):
            z_copy(way, r).wait_send()

    @pl.loop(0, part)
    def _(hd):
        for k in range(1, NX):
            in_copy(hd, k).wait_send()
            out_copy(hd, k).wait_send()


def sds(shape, kind=F32):
    return jax.ShapeDtypeStruct(shape, kind)


def whole(slots, dps, parent, alog, bias, skip, x, dy, raw, b, c):
    heads, t = raw.shape
    pairs = heads // 2
    groups = b.shape[1] // STATE
    part = heads // NX
    size = HEAD_DIM // PIECES
    rounds = part * PIECES + LAG * (ARM - 1)
    dma = pltpu.SemaphoreType.DMA
    vmem = pl.BlockSpec(memory_space=pltpu.VMEM)
    smem = pl.BlockSpec(memory_space=pltpu.SMEM)
    rows = pltpu.VMEM((pairs, 2, t), F32)
    turned = pltpu.VMEM((pairs, 2 * HEAD_DIM, t), BF16)
    return pl.pallas_call(
        functools.partial(whole_kernel, slots, dps),
        in_specs=[smem] * 4 + [vmem] * 5,
        out_specs=[vmem] * 5,
        out_shape=[
            sds((t, heads * HEAD_DIM), BF16),
            sds((heads, t)),
            sds((t, groups * STATE)),
            sds((t, groups * STATE)),
            sds((8, STATE)),
        ],
        scratch_shapes=[
            pltpu.VMEM((heads, t), F32),
            pltpu.VMEM((heads, t), F32),
            pltpu.VMEM((pairs, t, 2), F32),
            rows,
            rows,
            rows,
            pltpu.VMEM((t, t), BF16),
            pltpu.VMEM((groups, t, t), F32),
            pltpu.VMEM((groups, t, t), F32),
            pltpu.VMEM((groups, STATE, t), F32),
            pltpu.VMEM((groups, STATE, t), F32),
            turned,
            turned,
            pltpu.VMEM((pairs, 2 * HEAD_DIM, t), F32),
            rows,
            rows,
            pltpu.VMEM((heads, 2, HEAD_DIM, STATE), F32),
            pltpu.VMEM((heads, 2, HEAD_DIM, STATE), F32),
            pltpu.VMEM((dps, 1, STATE), F32),
            dma((dps,)),
            dma((dps,)),
            pltpu.VMEM((NX, part, 2, HEAD_DIM, STATE), F32),
            pltpu.VMEM((part, HEAD_DIM, STATE), F32),
            pltpu.VMEM((2, rounds + LAG, slots, size, STATE), F32),
            pltpu.VMEM((2, 3, slots, size, STATE), F32),
            pltpu.VMEM((NX, part, 2, HEAD_DIM, STATE), F32),
            pltpu.VMEM((1, 1, STATE), F32),
            pltpu.VMEM((NX * NZ, 1, STATE), F32),
            pltpu.VMEM((NX, heads, 1, STATE), F32),
            pltpu.VMEM((2, slots, slots, 1, STATE), F32),
            pltpu.VMEM((2, NX, slots, 1, STATE), F32),
            pltpu.VMEM((2, ARM, NX + 1, slots, 1, STATE), F32),
            pltpu.VMEM((NX, NX + 1, 1, STATE), F32),
            dma((part, NX - 1)),
            dma((part, NX - 1)),
            dma((2, 3)),
            dma((2, rounds)),
            dma((part, NX - 1)),
            dma((part, NX - 1)),
            dma((part,)),
            dma,
            dma,
        ],
        compiler_params=pltpu.CompilerParams(collective_id=slots, has_side_effects=True, vmem_limit_bytes=62 << 20),
        name=f"whole_{slots}",
    )(parent, alog, bias, skip, x, dy, raw, b, c)


def settle_kernel(n, *refs):
    for i in range(n):
        refs[n + i][...] = refs[i][...]


def settle(arrays):
    n, parts = len(arrays), 4
    spots = [pl.BlockSpec((a.shape[0] // parts, a.shape[1]), lambda i: (i, 0)) for a in arrays]
    return tuple(
        pl.pallas_call(
            functools.partial(settle_kernel, n),
            grid=(parts,),
            in_specs=spots,
            out_specs=spots,
            out_shape=[sds(a.shape, a.dtype) for a in arrays],
            name="settle",
        )(*arrays)
    )


FEW = 6
ALL = 13


def body(inputs, dt_raw, b_proj, c_proj, a_log, dt_bias, skip, grad_out, parent, children):
    given = (parent, a_log, dt_bias, skip, inputs[0], grad_out[0], dt_raw[0], b_proj[0], c_proj[0])
    dps = lax.axis_size("dp")
    *grads, most = whole(FEW, dps, *given)
    grads = lax.cond(most[0, 0] < FEW + 0.5, lambda: settle(grads), lambda: settle(whole(ALL, dps, *given)[:4]))
    return tuple(g[None] for g in grads)


def solution(mesh):
    placed = (
        P(("dp", "leaf"), None, "heads"),
        P(("dp", "leaf"), "heads", None),
        P(("dp", "leaf"), None, "heads"),
        P(("dp", "leaf"), None, "heads"),
        P("heads"),
        P("heads"),
        P("heads"),
        P(("dp", "leaf"), None, "heads"),
        P("dp"),
        P("dp", None),
    )
    return jax.shard_map(
        body,
        mesh=mesh,
        in_specs=placed,
        out_specs=(
            P(("dp", "leaf"), None, "heads"),
            P(("dp", "leaf"), "heads", None),
            P(("dp", "leaf"), None, "heads"),
            P(("dp", "leaf"), None, "heads"),
        ),
        check_vma=False,
    )
```

```python
import functools

import jax
import jax.numpy as jnp
from jax import lax
from jax.experimental import pallas as pl
from jax.experimental.pallas import tpu as pltpu
from jax.sharding import PartitionSpec as P

HEAD_DIM = 64
STATE = 128
NX = 4
NZ = 8
PIECES = 2
ARM = 5
LAG = 3
F32 = jnp.float32
BF16 = jnp.bfloat16

MESH = pl.DeviceIdType.MESH


def dot(a, b, da=1, db=0):
    return lax.dot_general(a, b, (((da,), (db,)), ((), ())), preferred_element_type=F32)


def prefix(rows, ones):
    top = rows.astype(BF16)
    rest = rows - top.astype(F32)
    mid = rest.astype(BF16)
    low = (rest - mid.astype(F32)).astype(BF16)
    return dot(top, ones) + (dot(mid, ones) + dot(low, ones))


def triangle(n, lower):
    r = lax.broadcasted_iota(jnp.int32, (n, n), 0)
    c = lax.broadcasted_iota(jnp.int32, (n, n), 1)
    return jnp.where(r >= c if lower else r <= c, 1.0, 0.0).astype(BF16)


def spread(rows, flat):
    h, t = rows.shape
    return (flat.astype(F32).reshape(h, -1, t) * rows[:, None, :]).reshape(flat.shape)


def fold(flat, heads):
    return flat.reshape(heads, -1, flat.shape[1]).sum(axis=1)


def scalars(ref, shape):
    row = lax.broadcasted_iota(jnp.int32, shape, 0)
    out = jnp.zeros(shape, F32)
    for h in range(shape[0]):
        out = jnp.where(row == h, ref[h], out)
    return out[:, :1]


def prepare(slots, alog_ref, bias_ref, raw_ref, b_ref, c_ref, rate_s, slope_s, rise_s, fall_s, tail_s, growth_s, ones_s, score, summed, sumb, sumc):
    heads, t = raw_ref.shape
    v = raw_ref[...] + scalars(bias_ref, (heads, STATE))
    rate = jnp.maximum(v, 0.0) + jnp.log1p(jnp.exp(-jnp.abs(v)))
    rate_s[...] = rate
    slope_s[...] = 1.0 / (1.0 + jnp.exp(-v))
    cum = prefix(-jnp.exp(scalars(alog_ref, (heads, STATE))) * rate, triangle(t, False))
    ones_s[...] = triangle(t, True)
    rise = cum.T
    fall = jnp.log(rate) - cum
    tail = jnp.exp(cum[:, -1:] - cum) * rate
    growth = jnp.exp(cum)
    for i in range(heads // 2):
        two = slice(2 * i, 2 * i + 2)
        rise_s[i] = rise[:, two]
        fall_s[i] = fall[two]
        tail_s[i] = tail[two]
        growth_s[i] = growth[two]
    for g in range(score.shape[0]):
        group = slice(g * STATE, (g + 1) * STATE)
        score[g] = dot(c_ref[:, group], b_ref[:, group], 1, 1)
    summed[...] = jnp.zeros_like(summed)
    sumb[...] = jnp.zeros_like(sumb)
    sumc[...] = jnp.zeros_like(sumc)
    return jnp.exp(rise[t - 1 :, :])


def columns(index, width):
    return pl.ds(pl.multiple_of(index * width, width), width)


def summary_pair(pair, group, x_ref, dy_ref, b_ref, c_ref, xt_s, dyt_s, tail_s, growth_s):
    mine = columns(pair, 2 * HEAD_DIM)
    xt = x_ref[:, mine].T
    dyt = dy_ref[:, mine].T
    xt_s[pair] = xt
    dyt_s[pair] = dyt
    end = dot(spread(tail_s[pair], xt).astype(BF16), b_ref[:, columns(group, STATE)])
    pull = dot(spread(growth_s[pair], dyt).astype(BF16), c_ref[:, columns(group, STATE)])
    return end.reshape(2, HEAD_DIM, STATE), pull.reshape(2, HEAD_DIM, STATE)


def inner_pair(pair, group, skip_ref, dy_ref, xt_s, dyt_s, rise_s, fall_s, dx_s, row_s, col_s, score, summed):
    t = dy_ref.shape[0]
    half = t // 2
    both = 2 * HEAD_DIM
    rise = rise_s[pair]
    fall = fall_s[pair]
    xpair = xt_s[pair]
    dypair = dyt_s[pair]
    dycols = dy_ref[:, columns(pair, both)]
    causal = lax.broadcasted_iota(jnp.int32, (half, half), 0) >= lax.broadcasted_iota(jnp.int32, (half, half), 1)
    where_x = lax.broadcasted_iota(jnp.int32, (both, t), 0) // HEAD_DIM
    lefts, downs, outs = [], [], []
    for i in range(2):
        xhead = jnp.where(where_x == i, xpair, jnp.zeros_like(xpair))
        dyh = dypair[i * HEAD_DIM : (i + 1) * HEAD_DIM]
        skip = skip_ref[2 * pair + i]
        parts = {}
        for a, b in ((0, 0), (1, 0), (1, 1)):
            rows = slice(a * half, (a + 1) * half)
            cols = slice(b * half, (b + 1) * half)
            gap = rise[rows, i : i + 1] + fall[i : i + 1, cols]
            if a == b:
                gap = jnp.where(causal, gap, -1e30)
            decay = jnp.exp(gap)
            mix = decay * score[group, rows, cols]
            dmix = dot(dycols[rows], xhead[:, cols])
            summed[group, rows, cols] += dmix * decay
            parts[a, b] = (mix.astype(BF16), dmix * mix)
        q0, q1, q2 = parts[0, 0][1], parts[1, 0][1], parts[1, 1][1]
        downs.append(
            jnp.concatenate([jnp.sum(q0 + q1, axis=0, keepdims=True), jnp.sum(q2, axis=0, keepdims=True)], axis=1)
        )
        lefts.append(
            jnp.concatenate([jnp.sum(q0, axis=1, keepdims=True), jnp.sum(q1 + q2, axis=1, keepdims=True)], axis=0)
        )
        left = jnp.concatenate([parts[0, 0][0], parts[1, 0][0]], axis=0)
        outs.append(
            jnp.concatenate([dot(dyh, left), dot(dyh[:, half:], parts[1, 1][0])], axis=1) + skip * dyh.astype(F32)
        )
    dx_s[pair] = jnp.concatenate(outs, axis=0)
    col_s[pair] = jnp.concatenate(downs, axis=0)
    row_s[pair] = jnp.concatenate(lefts, axis=1).T


def final_pair(pair, group, b_ref, c_ref, states, xt_s, dyt_s, tail_s, growth_s, dx_s, row_s, col_s, sumb, sumc, gx_ref):
    two = pl.ds(2 * pair, 2)
    start = states[two, 0].reshape(2 * HEAD_DIM, STATE)
    grad = states[two, 1].reshape(2 * HEAD_DIM, STATE)
    tail = tail_s[pair]
    growth = growth_s[pair]
    inner = jnp.sum(fold(start * grad, 2), axis=1, keepdims=True)
    start_low = start.astype(BF16)
    grad_low = grad.astype(BF16)
    xt = xt_s[pair]
    dyt = dyt_s[pair]
    own = columns(group, STATE)
    pulled = dot(grad_low, b_ref[:, own], 1, 1)
    z = fold(xt.astype(F32) * pulled, 2) * tail
    gx_ref[:, columns(pair, 2 * HEAD_DIM)] = (dx_s[pair] + spread(tail, pulled)).astype(BF16).T
    sumb[group] += dot(grad_low, spread(tail, xt).astype(BF16), 0, 0)
    carried = dot(start_low, c_ref[:, own], 1, 1)
    g = fold(dyt.astype(F32) * carried, 2) * growth
    sumc[group] += dot(start_low, spread(growth, dyt).astype(BF16), 0, 0)
    col = col_s[pair]
    at_end = jnp.sum(z, axis=1, keepdims=True) + growth[:, -1:] * inner
    lane = lax.broadcasted_iota(jnp.int32, z.shape, 1)
    row_s[pair] = row_s[pair] - col + g - z + jnp.where(lane == z.shape[1] - 1, at_end, 0.0)
    col_s[pair] = col + z


def finish(alog_ref, b_ref, c_ref, rate_s, slope_s, ones_s, row_s, col_s, summed, sumb, sumc, gdt_ref, gb_ref, gc_ref):
    heads, t = rate_s.shape
    dcum = jnp.concatenate([row_s[i] for i in range(heads // 2)], axis=0)
    dlog_rate = jnp.concatenate([col_s[i] for i in range(heads // 2)], axis=0)
    dlog = prefix(dcum, ones_s[...])
    gdt_ref[...] = (dlog_rate / rate_s[...] - jnp.exp(scalars(alog_ref, (heads, STATE))) * dlog) * slope_s[...]
    r = lax.broadcasted_iota(jnp.int32, (t, t), 0)
    c = lax.broadcasted_iota(jnp.int32, (t, t), 1)
    for g in range(summed.shape[0]):
        group = slice(g * STATE, (g + 1) * STATE)
        low = jnp.where(r >= c, summed[g], 0.0).astype(BF16)
        gb_ref[:, group] = (sumb[g] + dot(c_ref[:, group], low, 0, 0)).T
        gc_ref[:, group] = (sumc[g] + dot(b_ref[:, group], low, 0, 1)).T


def arms(near, sub, lane):
    pick = (lane - sub) & (NZ - 1)
    ups, downs, covers = [], [], []
    for k in range(NZ - ARM - 1, ARM + 1):
        up = jnp.max(jnp.where(near & (pick <= k), pick, 0), axis=1, keepdims=True)
        down = jnp.max(jnp.where(near & (pick > k), NZ - pick, 0), axis=1, keepdims=True)
        used = (((lane - sub) & (NZ - 1)) < up) | (((sub - 1 - lane) & (NZ - 1)) < down)
        ups.append(jnp.broadcast_to(up, sub.shape))
        downs.append(jnp.broadcast_to(down, sub.shape))
        covers.append(jnp.where(used & (lane < NZ), 1.0, 0.0))
    up, down, now = ups[0], downs[0], covers[0]
    least = jnp.sum(now, axis=1, keepdims=True)
    for k in range(1, len(covers)):
        steps = jnp.sum(covers[k], axis=1, keepdims=True)
        less = jnp.broadcast_to(steps < least, sub.shape)
        up, down, now = jnp.where(less, ups[k], up), jnp.where(less, downs[k], down), jnp.where(less, covers[k], now)
        least = jnp.minimum(steps, least)
    for _ in range(3):
        load = jnp.sum(now, axis=0, keepdims=True) - now
        costs = []
        for cover in covers:
            cost = jnp.where(lane < NZ, jnp.exp((load + cover) * 1.3862944), 0.0)
            costs.append(jnp.broadcast_to(jnp.sum(cost, axis=1, keepdims=True), sub.shape))
        best = functools.reduce(jnp.minimum, costs)
        best = jnp.min(best, axis=0, keepdims=True)
        names = [jnp.where(cost == best, k * NX * NZ + sub, NX * NZ * NZ) for k, cost in enumerate(costs)]
        name = jnp.min(functools.reduce(jnp.minimum, names), axis=0, keepdims=True)
        for k in range(len(covers)):
            hit = name == k * NX * NZ + sub
            up, down, now = jnp.where(hit, ups[k], up), jnp.where(hit, downs[k], down), jnp.where(hit, covers[k], now)
    return up, down


def whole_kernel(slots, dps, parent_ref, alog_ref, bias_ref, skip_ref, x_ref, dy_ref, raw_ref, b_ref, c_ref,
                 gx_ref, gdt_ref, gb_ref, gc_ref, most_ref,
                 rate_s, slope_s, rise_s, fall_s, tail_s, growth_s, ones_s, score, summed, sumb, sumc, xt_s, dyt_s, dx_s, row_s, col_s, own_ref, both_ref,
                 counts, count_send, count_recv, xin, extra, got, put, res, crow, carried, scale, relay, local, remote, here,
                 in_send, in_recv, z_send, z_recv, out_send, out_recv, out_own, carry_send, carry_recv):
    nodes = NX * NZ
    part = own_ref.shape[0] // NX
    size = HEAD_DIM // PIECES
    chunks = part * PIECES
    rounds = chunks + LAG * (ARM - 1)
    pairs = own_ref.shape[0] // 2
    groups = score.shape[0]
    first = 2 * NX
    me = lax.axis_index("leaf")
    x, z = me // NZ, lax.rem(me, NZ)

    def peer(k):
        return lax.rem(x + k, NX)

    def at(px, pz):
        return {"leaf": px * NZ + pz}

    barrier = pltpu.get_barrier_semaphore()
    tree_at = lax.axis_index("dp")
    for k in range(1, dps):
        pl.semaphore_signal(barrier, inc=1, device_id={"dp": lax.rem(tree_at + k, dps)}, device_id_type=MESH)

    @pl.loop(1, nodes)
    def _(k):
        pl.semaphore_signal(barrier, inc=1, device_id={"leaf": lax.rem(me + k, nodes)}, device_id_type=MESH)

    crow[...] = jnp.zeros_like(crow)
    crow[0, :, : own_ref.shape[0]] = prepare(
        slots, alog_ref, bias_ref, raw_ref, b_ref, c_ref, rate_s, slope_s, rise_s, fall_s, tail_s, growth_s, ones_s, score, summed, sumb, sumc
    )
    got[:, 0:LAG] = jnp.zeros((2, LAG) + got.shape[2:], F32)

    def place(index):
        side = lax.rem(index, NX)
        pair = side * (pairs // NX) + index // NX
        return pair, side, pair // (pairs // groups)

    def summary(index):
        pair, side, group = place(index)
        end, pull = summary_pair(pair, group, x_ref, dy_ref, b_ref, c_ref, xt_s, dyt_s, tail_s, growth_s)
        own_ref[pl.ds(2 * pair, 2), 0] = end
        own_ref[pl.ds(2 * pair, 2), 1] = pull

        @pl.when(side == x)
        def _():
            hd = pl.ds(2 * (index // NX), 2)
            xin[x, hd, 0] = end
            xin[x, hd, 1] = pull

    @pl.loop(0, first)
    def _(index):
        summary(index)

    pl.semaphore_wait(barrier, nodes + dps - 2)

    def in_copy(hd, k):
        return pltpu.make_async_remote_copy(
            src_ref=own_ref.at[peer(k) * part + hd],
            dst_ref=xin.at[x, hd],
            send_sem=in_send.at[hd, k - 1],
            recv_sem=in_recv.at[hd, k - 1],
            device_id=at(peer(k), z),
            device_id_type=MESH,
        )

    def start_in(hd):
        for k in range(1, NX):
            in_copy(hd, k).start()

    start_in(0)

    def carry_copy(k):
        return pltpu.make_async_remote_copy(
            src_ref=crow.at[0],
            dst_ref=carried.at[me],
            send_sem=carry_send,
            recv_sem=carry_recv,
            device_id={"leaf": lax.rem(me + k, nodes)},
            device_id_type=MESH,
        )

    @pl.loop(1, nodes)
    def _(k):
        carry_copy(k).start()

    for hd in range(1, 2 * first // NX):
        start_in(hd)

    lanes = 128
    sub = lax.broadcasted_iota(jnp.int32, (nodes, lanes), 0)
    lane = lax.broadcasted_iota(jnp.int32, (nodes, lanes), 1)
    par_col = jnp.full((nodes, lanes), -1, jnp.int32)
    par_row = jnp.full((nodes, lanes), -2, jnp.int32)
    for n in range(nodes):
        par_col = jnp.where(sub == n, parent_ref[n], par_col)
        par_row = jnp.where(lane == n, parent_ref[n], par_row)
    is_root = par_col < 0
    near = (par_row == sub) | (is_root & (lane < nodes))
    up, down = arms(near, sub, lane)

    def one(v):
        return jnp.where(v, 1.0, 0.0)

    order = one(lax.broadcasted_iota(jnp.int32, (nodes, nodes), 0) > lax.broadcasted_iota(jnp.int32, (nodes, nodes), 1))

    def users(e):
        return ((e - sub) & (NZ - 1)) < up, ((sub - 1 - e) & (NZ - 1)) < down

    def used_by(e):
        rising, falling = users(e)
        return one(rising | falling)

    def edge(e):
        rising, falling = users(e)
        used = used_by(e)
        rank = dot(order, used)
        slot = lax.broadcasted_iota(jnp.int32, (slots, nodes, lanes), 0).astype(F32)
        place = jnp.where(jnp.abs(slot - rank[None]) < 0.5, used[None], 0.0)
        return one(rising), one(falling), place

    busy = jnp.zeros((1, lanes), F32)
    for e in range(NZ):
        busy = jnp.maximum(busy, jnp.sum(used_by(e), axis=0, keepdims=True))
    counts[tree_at] = busy

    def count_copy(k):
        return pltpu.make_async_remote_copy(
            src_ref=counts.at[tree_at],
            dst_ref=counts.at[tree_at],
            send_sem=count_send.at[k - 1],
            recv_sem=count_recv.at[k - 1],
            device_id={"dp": lax.rem(tree_at + k, dps)},
            device_id_type=MESH,
        )

    for k in range(1, dps):
        count_copy(k).start()

    up_in, down_in, place_in = edge(z + NZ - 1)
    up_out, down_out, place_out = edge(z)

    def total(v):
        return jnp.sum(v, axis=1, keepdims=True)

    same = up_in * up_out + down_in * down_out
    for j in range(slots):
        relay[0, j] = total(place_out * (place_in[j] * same)[None])
        relay[1, j] = total(place_in * (place_out[j] * same)[None])
    wants = [one(sub == parent_ref[k * NZ + z]) for k in range(NX)] + [one(is_root)]
    for k in range(NX):
        mine = one(sub == k * NZ + z)
        local[0, k] = total(place_out * (up_out * mine)[None])
        local[1, k] = total(place_in * (down_in * mine)[None])
        for m in range(NX + 1):
            here[k, m] = jnp.sum(wants[m] * mine, axis=0, keepdims=True)
    for d in range(ARM):
        far_up = one(((z - sub) & (NZ - 1)) == d + 1) * up_in
        far_down = one(((sub - z) & (NZ - 1)) == d + 1) * down_out
        for m in range(NX + 1):
            remote[0, d, m] = total(place_in * (far_up * wants[m])[None])
            remote[1, d, m] = total(place_out * (far_down * wants[m])[None])

    for kind in ("send", "recv"):
        rows = carried.at[0 : nodes - 1]
        wait = pltpu.make_async_copy(rows, rows, carry_send if kind == "send" else carry_recv)
        wait.wait()
    carried[me] = crow[0]
    decays = carried[:, 0, :]
    for k in range(NX):
        row = jnp.sum(jnp.where(is_root, 0.0, wants[k] * decays), axis=0, keepdims=True)
        scale[k] = jnp.broadcast_to(row, (lanes, lanes)).T[: scale.shape[1], None, :]
    def z_copy(way, r):
        to = lax.rem(z + (1 if way == 0 else NZ - 1), NZ)
        return pltpu.make_async_remote_copy(
            src_ref=put.at[way, lax.rem(r, 3)],
            dst_ref=got.at[way, r + LAG],
            send_sem=z_send.at[way, lax.rem(r, 3)],
            recv_sem=z_recv.at[way, r],
            device_id=at(x, to),
            device_id_type=MESH,
        )

    def out_copy(hd, k):
        return pltpu.make_async_remote_copy(
            src_ref=res.at[peer(k), hd],
            dst_ref=both_ref.at[x * part + hd],
            send_sem=out_send.at[hd, k - 1],
            recv_sem=out_recv.at[hd, k - 1],
            device_id=at(peer(k), z),
            device_id_type=MESH,
        )

    def own_out(hd):
        return pltpu.make_async_copy(res.at[x, hd], both_ref.at[x * part + hd], out_own.at[hd])

    def part_of(chunk):
        return pl.ds(pl.multiple_of(lax.rem(chunk, PIECES) * size, size), size)

    def piece(k, chunk, kind):
        return xin[k, chunk // PIECES, kind, part_of(chunk), :]

    last = LAG * ARM

    late = last + 2 * NX - 2

    @pl.loop(0, pairs + late)
    def _(r):
        @pl.when((r >= LAG) & (r < rounds + LAG))
        def _():
            for way in range(2):
                z_copy(way, r - LAG).wait_recv()

        @pl.when((lax.rem(r, PIECES) == 0) & (r < chunks))
        def _():
            hd = r // PIECES

            for k in range(1, NX):
                in_copy(hd, k).wait_recv()
            summed = scale[0, x * part + hd] * xin[0, hd, 1]
            for k in range(1, NX):
                summed += scale[k, x * part + hd] * xin[k, hd, 1]
            extra[hd] = summed

        @pl.when(r < rounds)
        def _():
            @pl.when(r >= 3)
            def _():
                for way in range(2):
                    z_copy(way, r - 3).wait_send()

            for way in range(2):
                now = jnp.minimum(r, chunks - 1)
                acc = local[way, 0] * piece(0, now, 0)[None]
                for k in range(1, NX):
                    acc += local[way, k] * piece(k, now, 0)[None]
                for d in range(ARM):
                    chunk = jnp.clip(r - LAG * (ARM - 1 - d), 0, chunks - 1)
                    for k in range(NX):
                        acc += remote[1 - way, d, k] * piece(k, chunk, 1)[None]
                    acc += remote[1 - way, d, NX] * extra[chunk // PIECES, part_of(chunk), :][None]
                for j in range(slots):
                    acc += relay[way, j] * got[way, r, j][None]
                put[way, lax.rem(r, 3)] = acc
                z_copy(way, r).start()

        @pl.when((r >= last) & (r < chunks + last))
        def _():
            c = r - last
            hd = c // PIECES
            rows = part_of(c)
            begin = here[0] * piece(0, c, 0)[None]
            for k in range(1, NX):
                begin += here[k] * piece(k, c, 0)[None]
            for way in range(2):
                for d in range(ARM):
                    for j in range(slots):
                        begin += remote[way, d, :, j] * got[way, c + LAG * (d + 1), j][None]
            end = here[:, NX] * extra[hd, rows, :][None]
            for k in range(NX):
                end += here[:, k] * piece(k, c, 1)[None]
            for way in range(2):
                for j in range(slots):
                    end += local[1 - way, :, j] * got[way, c + LAG * ARM, j][None]
            for k in range(NX):
                res[k, hd, 0, rows, :] = begin[k] + scale[k, x * part + hd] * begin[NX]
                res[k, hd, 1, rows, :] = end[k]

            @pl.when(lax.rem(c, PIECES) == PIECES - 1)
            def _():
                for k in range(1, NX):
                    out_copy(hd, k).start()
                own_out(hd).start()

        @pl.when(r + first < pairs)
        def _():
            summary(r + first)

            @pl.when(lax.rem(r + first, NX) == NX - 1)
            def _():
                start_in(2 * ((r + first) // NX))
                start_in(2 * ((r + first) // NX) + 1)

        @pl.when(r < pairs)
        def _():
            pair, side, group = place(r)
            inner_pair(pair, group, skip_ref, dy_ref, xt_s, dyt_s, rise_s, fall_s, dx_s, row_s, col_s, score, summed)

        @pl.when(r >= late)
        def _():
            index = r - late

            @pl.when(lax.rem(index, NX) == 0)
            def _():
                for one_of in range(2):
                    hd = 2 * (index // NX) + one_of
                    for k in range(1, NX):
                        out_copy(hd, k).wait_recv()
                    own_out(hd).wait()

            pair, side, group = place(index)
            final_pair(pair, group, b_ref, c_ref, both_ref, xt_s, dyt_s, tail_s, growth_s, dx_s, row_s, col_s, sumb, sumc, gx_ref)

    finish(alog_ref, b_ref, c_ref, rate_s, slope_s, ones_s, row_s, col_s, summed, sumb, sumc, gdt_ref, gb_ref, gc_ref)
    for k in range(1, dps):
        count_copy(k).wait()
    most = counts[0]
    for k in range(1, dps):
        most = jnp.maximum(most, counts[k])
    most_ref[...] = jnp.broadcast_to(most, most_ref.shape)
    for way in range(2):
        for r in range(rounds - 3, rounds):
            z_copy(way, r).wait_send()

    @pl.loop(0, part)
    def _(hd):
        for k in range(1, NX):
            in_copy(hd, k).wait_send()
            out_copy(hd, k).wait_send()


def sds(shape, kind=F32):
    return jax.ShapeDtypeStruct(shape, kind)


def whole(slots, dps, parent, alog, bias, skip, x, dy, raw, b, c):
    heads, t = raw.shape
    pairs = heads // 2
    groups = b.shape[1] // STATE
    part = heads // NX
    size = HEAD_DIM // PIECES
    rounds = part * PIECES + LAG * (ARM - 1)
    dma = pltpu.SemaphoreType.DMA
    vmem = pl.BlockSpec(memory_space=pltpu.VMEM)
    smem = pl.BlockSpec(memory_space=pltpu.SMEM)
    rows = pltpu.VMEM((pairs, 2, t), F32)
    turned = pltpu.VMEM((pairs, 2 * HEAD_DIM, t), BF16)
    return pl.pallas_call(
        functools.partial(whole_kernel, slots, dps),
        in_specs=[smem] * 4 + [vmem] * 5,
        out_specs=[vmem] * 5,
        out_shape=[
            sds((t, heads * HEAD_DIM), BF16),
            sds((heads, t)),
            sds((t, groups * STATE)),
            sds((t, groups * STATE)),
            sds((8, STATE)),
        ],
        scratch_shapes=[
            pltpu.VMEM((heads, t), F32),
            pltpu.VMEM((heads, t), F32),
            pltpu.VMEM((pairs, t, 2), F32),
            rows,
            rows,
            rows,
            pltpu.VMEM((t, t), BF16),
            pltpu.VMEM((groups, t, t), F32),
            pltpu.VMEM((groups, t, t), F32),
            pltpu.VMEM((groups, STATE, t), F32),
            pltpu.VMEM((groups, STATE, t), F32),
            turned,
            turned,
            pltpu.VMEM((pairs, 2 * HEAD_DIM, t), F32),
            rows,
            rows,
            pltpu.VMEM((heads, 2, HEAD_DIM, STATE), F32),
            pltpu.VMEM((heads, 2, HEAD_DIM, STATE), F32),
            pltpu.VMEM((dps, 1, STATE), F32),
            dma((dps,)),
            dma((dps,)),
            pltpu.VMEM((NX, part, 2, HEAD_DIM, STATE), F32),
            pltpu.VMEM((part, HEAD_DIM, STATE), F32),
            pltpu.VMEM((2, rounds + LAG, slots, size, STATE), F32),
            pltpu.VMEM((2, 3, slots, size, STATE), F32),
            pltpu.VMEM((NX, part, 2, HEAD_DIM, STATE), F32),
            pltpu.VMEM((1, 1, STATE), F32),
            pltpu.VMEM((NX * NZ, 1, STATE), F32),
            pltpu.VMEM((NX, heads, 1, STATE), F32),
            pltpu.VMEM((2, slots, slots, 1, STATE), F32),
            pltpu.VMEM((2, NX, slots, 1, STATE), F32),
            pltpu.VMEM((2, ARM, NX + 1, slots, 1, STATE), F32),
            pltpu.VMEM((NX, NX + 1, 1, STATE), F32),
            dma((part, NX - 1)),
            dma((part, NX - 1)),
            dma((2, 3)),
            dma((2, rounds)),
            dma((part, NX - 1)),
            dma((part, NX - 1)),
            dma((part,)),
            dma,
            dma,
        ],
        compiler_params=pltpu.CompilerParams(collective_id=slots, has_side_effects=True, vmem_limit_bytes=62 << 20),
        name=f"whole_{slots}",
    )(parent, alog, bias, skip, x, dy, raw, b, c)


def settle_kernel(n, *refs):
    for i in range(n):
        refs[n + i][...] = refs[i][...]


def settle(arrays):
    n, parts = len(arrays), 4
    spots = [pl.BlockSpec((a.shape[0] // parts, a.shape[1]), lambda i: (i, 0)) for a in arrays]
    return tuple(
        pl.pallas_call(
            functools.partial(settle_kernel, n),
            grid=(parts,),
            in_specs=spots,
            out_specs=spots,
            out_shape=[sds(a.shape, a.dtype) for a in arrays],
            name="settle",
        )(*arrays)
    )


FEW = 6
ALL = 13


def body(inputs, dt_raw, b_proj, c_proj, a_log, dt_bias, skip, grad_out, parent, children):
    given = (parent, a_log, dt_bias, skip, inputs[0], grad_out[0], dt_raw[0], b_proj[0], c_proj[0])
    dps = lax.axis_size("dp")
    *grads, most = whole(FEW, dps, *given)
    grads = lax.cond(most[0, 0] < FEW + 0.5, lambda: settle(grads), lambda: settle(whole(ALL, dps, *given)[:4]))
    return tuple(g[None] for g in grads)


def solution(mesh):
    placed = (
        P(("dp", "leaf"), None, "heads"),
        P(("dp", "leaf"), "heads", None),
        P(("dp", "leaf"), None, "heads"),
        P(("dp", "leaf"), None, "heads"),
        P("heads"),
        P("heads"),
        P("heads"),
        P(("dp", "leaf"), None, "heads"),
        P("dp"),
        P("dp", None),
    )
    return jax.shard_map(
        body,
        mesh=mesh,
        in_specs=placed,
        out_specs=(
            P(("dp", "leaf"), None, "heads"),
            P(("dp", "leaf"), "heads", None),
            P(("dp", "leaf"), None, "heads"),
            P(("dp", "leaf"), None, "heads"),
        ),
        check_vma=False,
    )
```
